32 devices in a mesh: ep: 4 (over y, x), tm: 8 (over z, core).
Axes of the slice: x: 2, y: 2, z: 4, core: 2. Of those that a mesh axis runs over, the one named last changes fastest.
Arguments:
- predictions: float32 [128, 262144], P('ep', 'tm'), may hold values from -6 to 6
- leaf_index: int32 [128, 262144], P('ep', 'tm'), may hold values from 0 to 63
- events: int32 [128, 262144], P('ep', 'tm'), may hold values 0 or 1
- tie_start: int32 [262144], P('tm'), may hold values from 0 to 1, as said below
Outputs:
- new_pred: float32 [128, 262144], P('ep', 'tm')
- leaf_weights: float32 [128, 64], P('ep')
- grad_hess: bfloat16 [2, 128, 8, 32768], P(None, None, 'tm', 'ep')
The draws below stay inside these ranges and needn't reach their ends.
Inputs may be any that keep to these rules, and one draw needn't show every extreme that they name: `tie_start`: every row whose index is a multiple of 128 begins a tie group.
All inputs are finite; a program needn't handle non-finite values. No bound on the sum of `events` on one device may be relied on, other than what follows from the above.
Results may differ from the reference program's by a relative error of at most 0.0023.
Values may be sent and summed in bfloat16 or wider, within the bound.
No kernel may reach another device: no remote copies, remote signals or barrier semaphores. Data moves between devices by JAX's collectives and lax.ppermute only.
A program may use at most 128 MiB of HBM per device.

```python
import jax
import jax.numpy as jnp
from jax import lax

ENDPOINTS = 128
LEAVES = 64
ROWS_DEV = 32768
ROWS = 262144
N_TM = 8


def draw_tie_start(key, part):
    positions = jnp.arange(ROWS_DEV * N_TM, dtype=jnp.int32)
    coins = (jax.random.randint(key, (ROWS_DEV * N_TM,), 0, 16) == 0).astype(jnp.int32)
    return jnp.where(positions % 128 == 0, 1, coins).astype(jnp.int32)


def draw_predictions(key, part):
    rows_all = ROWS_DEV * N_TM
    noise_key = jax.random.fold_in(key, 11)
    spike_key = jax.random.fold_in(key, 23)
    place = jnp.arange(rows_all, dtype=jnp.float32) / jnp.float32(rows_all)
    noise = jax.random.normal(noise_key, (ENDPOINTS, rows_all), jnp.float32)
    level = -3.0 * place * place
    spikes = (jax.random.randint(spike_key, (ENDPOINTS, rows_all), 0, 512) == 0).astype(jnp.float32)
    return jnp.clip(level[None, :] + noise + 5.0 * spikes, -6.0, 6.0).astype(jnp.float32)


def with_ends(result, own_key, least, largest):
    spot = [jax.random.randint(jax.random.fold_in(own_key, axis), (), 0, length) for axis, length in enumerate(result.shape)]
    longest = result.shape.index(max(result.shape))
    next_to = spot[:longest] + [(spot[longest] + 1) % result.shape[longest]] + spot[longest + 1:]
    return result.at[tuple(spot)].set(least).at[tuple(next_to)].set(largest)


def setup_inputs(seed: int = 0) -> dict:
    streams_of = jax.random.split(jax.random.key(seed), 5)
    predictions = draw_predictions(jax.random.fold_in(streams_of[4], 71), 0)
    leaf_index = with_ends(jax.random.randint(streams_of[1], (ENDPOINTS, ROWS), 0, LEAVES), jax.random.fold_in(streams_of[1], 1), 0, LEAVES - 1).astype(jnp.int32)
    events = with_ends((jax.random.randint(streams_of[2], (ENDPOINTS, ROWS), 0, 3) < 1).astype(jnp.int32), jax.random.fold_in(streams_of[2], 1), 0, 1)
    tie_start = draw_tie_start(jax.random.fold_in(streams_of[4], 71), 0)
    return {"predictions": predictions, "leaf_index": leaf_index, "events": events, "tie_start": tie_start}


def reference(predictions, leaf_index, events, tie_start):
    rows_all = tie_start.shape[0]
    positions = jnp.arange(rows_all, dtype=jnp.int32)
    first_row = lax.cummax(jnp.where(tie_start == 1, positions, 0).astype(jnp.int32), axis=0)
    next_start = jnp.concatenate([tie_start[1:], jnp.ones((1,), jnp.int32)])
    last_row = lax.cummin(jnp.where(next_start == 1, positions, rows_all - 1).astype(jnp.int32), axis=0, reverse=True)

    def endpoint(packed):
        pred_row, leaf_row, event_row = packed
        weight = jnp.exp(pred_row)
        suffix = jnp.cumsum(weight[::-1])[::-1]
        risk = suffix[first_row]
        observed = event_row.astype(jnp.float32)
        inv_one = observed / risk
        inv_two = inv_one / risk
        accum_one = jnp.cumsum(inv_one)[last_row]
        accum_two = jnp.cumsum(inv_two)[last_row]
        gradient = weight * accum_one - observed
        hessian = weight * accum_one - weight * weight * accum_two
        gsum = jax.ops.segment_sum(gradient, leaf_row, num_segments=LEAVES)
        hsum = jax.ops.segment_sum(hessian, leaf_row, num_segments=LEAVES)
        leaf_w = -gsum / (hsum + 1.0)
        updated = pred_row + leaf_w[leaf_row]
        return updated, leaf_w, gradient.astype(jnp.bfloat16), hessian.astype(jnp.bfloat16)

    new_pred, leaf_weights, gradients, hessians = lax.map(endpoint, (predictions, leaf_index, events))
    grad_hess = jnp.stack([gradients, hessians]).reshape(2, ENDPOINTS, N_TM, ROWS_DEV)
    return new_pred, leaf_weights, grad_hess
```

```python
import functools

import jax
import jax.numpy as jnp
from jax import lax
from jax.experimental import pallas as pl
from jax.experimental.pallas import tpu as pltpu
from jax.sharding import PartitionSpec as P

LEAVES = 64
LANES = 128
WIDE = 256
PARAMS = pltpu.CompilerParams(vmem_limit_bytes=24 * 1024 * 1024)
F32 = jnp.float32
BF16 = jnp.bfloat16


def resident(shape, dtype):
    return pltpu.VMEM(shape, dtype)


def near(array):
    return pltpu.with_memory_space_constraint(array, pltpu.VMEM)


def call(body, outs, *args, scratch=(), name=None):
    spec = pl.BlockSpec(memory_space=pltpu.VMEM)
    smem = pl.BlockSpec(memory_space=pltpu.SMEM)
    return pl.pallas_call(
        body,
        out_shape=outs,
        in_specs=[smem if a.ndim == 1 else spec for a in args],
        out_specs=[spec] * len(outs),
        scratch_shapes=list(scratch),
        compiler_params=PARAMS,
        name=name,
    )(*args)


def lane_sum(x):
    return jnp.broadcast_to(jnp.sum(x, axis=1, keepdims=True), (x.shape[0], LANES))


def fold(x):
    parts = [x[:, k : k + LANES] for k in range(0, x.shape[1], LANES)]
    while len(parts) > 1:
        parts = [a + b for a, b in zip(parts[::2], parts[1::2])] + parts[len(parts) & ~1 :]
    return parts[0]


def weights_body(pred, weight, total):
    rows, length = pred.shape
    step = min(length, 1024)

    def one(turn, acc):
        at = pl.ds(pl.multiple_of(turn * step, step), step)
        value = jnp.exp(pred[:, at])
        weight[:, at] = value
        return acc + fold(value)

    acc = lax.fori_loop(0, length // step, one, jnp.zeros((rows, LANES), F32), unroll=2)
    total[...] = lane_sum(acc)


def pair_dot(x, matrix):
    high = x.astype(BF16)
    low = (x - high.astype(F32)).astype(BF16)
    return jnp.dot(high, matrix, preferred_element_type=F32) + jnp.dot(low, matrix, preferred_element_type=F32)


def take(x, index):
    return jnp.take_along_axis(x, index, axis=1, mode="promise_in_bounds")


def tie_index(starts, from_end):
    lane = lax.broadcasted_iota(jnp.int32, starts.shape, 1)
    if not from_end:
        best = jnp.where(starts == 1, lane, 0)
        for shift in (1, 2, 4, 8, 16, 32, 64):
            moved = pltpu.roll(best, shift, 1)
            best = jnp.where(lane >= shift, jnp.maximum(best, moved), best)
        return best
    after = pltpu.roll(starts, LANES - 1, 1)
    best = jnp.where((after == 1) | (lane == LANES - 1), lane, LANES - 1)
    for shift in (1, 2, 4, 8, 16, 32, 64):
        moved = pltpu.roll(best, LANES - shift, 1)
        best = jnp.where(lane < LANES - shift, jnp.minimum(best, moved), best)
    return best


def stacked(ref, base, count, square=False):
    parts = [ref[:, pl.ds(pl.multiple_of(base + k * WIDE, WIDE), WIDE)] for k in range(count)]
    x = jnp.concatenate(parts, axis=0)
    return x * x if square else x


def scan_piece(out, index, summed, carry, base, rows, count, backward):
    order = range(count - 1, -1, -1) if backward else range(count)
    edge = 0 if backward else WIDE - 1
    for k in order:
        piece = summed[k * rows : (k + 1) * rows]
        for half in (0, 1):
            at = pl.multiple_of(base + k * WIDE + half * LANES, LANES)
            block = (base + k * WIDE) // LANES + half
            chosen = jnp.broadcast_to(index[pl.ds(block, 1), :], (rows, LANES))
            out[:, pl.ds(at, LANES)] = take(piece[:, half * LANES : (half + 1) * LANES], chosen) + carry
        carry = carry + jnp.broadcast_to(piece[:, edge : edge + 1], (rows, LANES))
    return carry


def risk_body(weight, tie, risk, last, first):
    rows, length = weight.shape
    count = min(8, length // WIDE)
    first[...] = tie_index(tie[...], False)
    last[...] = tie_index(tie[...], True)
    matrix = (lax.broadcasted_iota(jnp.int32, (WIDE, WIDE), 0) >= lax.broadcasted_iota(jnp.int32, (WIDE, WIDE), 1)).astype(BF16)
    steps = length // (WIDE * count)

    def one(turn, carry):
        base = (steps - 1 - turn) * (WIDE * count)
        summed = pair_dot(stacked(weight, base, count), matrix)
        return scan_piece(risk, first, summed, carry, base, rows, count, True)

    lax.fori_loop(0, steps, one, jnp.zeros((rows, LANES), F32))


def gathered_sum(masks, refs):
    out = None
    for k, ref in enumerate(refs):
        term = ref[...] * masks[k]
        out = term if out is None else out + term
    return out


def inverse_body(count, *refs):
    masks, others = refs[0], refs[1 : 1 + count]
    risk, events, inv, totals = refs[1 + count :]
    rows, length = risk.shape
    later = gathered_sum(masks, others)
    step = min(length, 512)

    def one(turn, acc):
        sum_one, sum_two = acc
        at = pl.ds(pl.multiple_of(turn * step, step), step)
        offset = jnp.concatenate([later] * (step // LANES), axis=1)
        value = events[:, at].astype(F32) / (risk[:, at] + offset)
        inv[:, at] = value
        return (sum_one + fold(value), sum_two + fold(value * value))

    empty = jnp.zeros((rows, LANES), F32)
    sum_one, sum_two = lax.fori_loop(0, length // step, one, (empty, empty))
    totals[:rows, :] = lane_sum(sum_one)
    totals[rows:, :] = lane_sum(sum_two)


def accum_body(inv, last, one_out, two_out):
    rows, length = inv.shape
    count = min(8, length // WIDE)
    matrix = (lax.broadcasted_iota(jnp.int32, (WIDE, WIDE), 0) <= lax.broadcasted_iota(jnp.int32, (WIDE, WIDE), 1)).astype(BF16)

    def one(turn, carry):
        base = turn * (WIDE * count)
        values = stacked(inv, base, count)
        first = scan_piece(one_out, last, pair_dot(values, matrix), carry[0], base, rows, count, False)
        second = scan_piece(two_out, last, pair_dot(values * values, matrix), carry[1], base, rows, count, False)
        return (first, second)

    empty = jnp.zeros((rows, LANES), F32)
    lax.fori_loop(0, length // (WIDE * count), one, (empty, empty))


def derivatives(weight, observed, accum_one, accum_two):
    scaled = weight * accum_one
    return scaled - observed, scaled - weight * weight * accum_two


def pieces_body(count, parts, *refs):
    masks, starts, others = refs[0], refs[1], refs[2 : 2 + count]
    weight, events, local_one, local_two = refs[2 + count : 6 + count]
    outs = refs[6 + count : 6 + count + parts]
    bases = refs[6 + count + parts]
    rows = weight.shape[0]
    length = outs[0].shape[2]
    earlier = gathered_sum(masks, others)
    bases[...] = earlier
    step = min(length, 512)

    for part in range(parts):

        def one(turn, carry):
            base_one = jnp.concatenate([bases[:rows, :]] * (step // LANES), axis=1)
            base_two = jnp.concatenate([bases[rows:, :]] * (step // LANES), axis=1)
            source = pl.ds(pl.multiple_of(starts[part] + turn * step, step), step)
            at = pl.ds(pl.multiple_of(turn * step, step), step)
            grad, hess = derivatives(
                weight[:, source],
                events[:, source].astype(F32),
                local_one[:, source] + base_one,
                local_two[:, source] + base_two,
            )
            outs[part][0, :, at] = grad.astype(BF16)
            outs[part][1, :, at] = hess.astype(BF16)
            return carry

        lax.fori_loop(0, length // step, one, 0)


GROUP = 16
LOW = 16
HIGH = LEAVES // LOW


def leaf_sums_body(leaf, weight, events, local_one, local_two, bases, sums, acc):
    rows, length = weight.shape
    step = min(length, 512)
    groups = rows // GROUP
    acc[...] = jnp.zeros_like(acc)

    def one(turn, carry):
        at = pl.ds(pl.multiple_of(turn * step, step), step)
        for group in range(groups):
            mine = pl.ds(group * GROUP, GROUP)
            base_one = jnp.concatenate([bases[mine, :]] * (step // LANES), axis=1)
            base_two = jnp.concatenate([bases[pl.ds(rows + group * GROUP, GROUP), :]] * (step // LANES), axis=1)
            pair = derivatives(
                weight[mine, at],
                events[mine, at].astype(F32),
                local_one[mine, at] + base_one,
                local_two[mine, at] + base_two,
            )
            label = leaf[mine, at]
            low = (label & (LOW - 1)).astype(F32).astype(BF16)
            high = (label // LOW).astype(F32).astype(BF16)
            terms = []
            for value in pair:
                upper = value.astype(BF16)
                terms += [upper, (value - upper.astype(F32)).astype(BF16)]
            zero = jnp.zeros((GROUP, step), BF16)
            unit = jnp.ones((GROUP, step), BF16)
            left = jnp.concatenate([jnp.where(high == h, term, zero) for term in terms for h in range(HIGH)], axis=0)
            right = jnp.concatenate([jnp.where(low == k, unit, zero) for k in range(LOW)], axis=0)
            acc[group] += lax.dot_general(left, right, (((1,), (1,)), ((), ())), preferred_element_type=F32)
        return carry

    lax.fori_loop(0, length // step, one, 0)
    width = LOW * GROUP
    side = HIGH * GROUP
    row_of = lax.broadcasted_iota(jnp.int32, (side, width), 0) % GROUP
    column_of = lax.broadcasted_iota(jnp.int32, (side, width), 1) % GROUP
    same = row_of == column_of
    source = lax.broadcasted_iota(jnp.int32, (width, LANES), 0) // GROUP
    target = lax.broadcasted_iota(jnp.int32, (width, LANES), 1)
    for group in range(groups):
        out = jnp.zeros((GROUP, LANES), F32)
        for value in (0, 1):
            both = acc[group, 2 * value * side : (2 * value + 1) * side] + acc[group, (2 * value + 1) * side : (2 * value + 2) * side]
            both = jnp.where(same, both, 0.0)
            for h in range(HIGH):
                place = (target == source + (h * LOW + value * LEAVES)).astype(F32)
                out = out + jnp.dot(
                    both[h * GROUP : (h + 1) * GROUP], place, precision=lax.Precision.HIGHEST, preferred_element_type=F32
                )
        sums[group * GROUP : (group + 1) * GROUP, :] = out


def update_body(pred, leaf, sums, new_pred, leaf_weights):
    rows, length = pred.shape
    both = sums[...]
    table = -both / (pltpu.roll(both, LANES - LEAVES, 1) + 1.0)
    leaf_weights[...] = table[:, :LEAVES]
    step = min(length, 512)

    def one(turn, carry):
        for k in range(step // LANES):
            at = pl.ds(pl.multiple_of(turn * step + k * LANES, LANES), LANES)
            new_pred[:, at] = pred[:, at] + take(table, leaf[:, at])
        return carry

    lax.fori_loop(0, length // step, one, 0)


def across(total, axis, fold_pairs):
    size = lax.axis_size(axis)
    mate = lax.ppermute(total, axis, [(i, i ^ 1) for i in range(size)])
    both = total + mate
    rest = [lax.ppermute(both, axis, [(i, i ^ d) for i in range(size)]) for d in range(2, size, 2)]
    return both, [mate] + rest


def masks_for(axis, later):
    size = lax.axis_size(axis)
    place = lax.axis_index(axis)
    others = [place ^ 1] + [place ^ d for d in range(2, size, 2)]
    wanted = [(o > place) if later else (o < place) for o in others]
    return jnp.stack(wanted).astype(F32)


def on_device(predictions, leaf_index, events, tie_start):
    rows, length = predictions.shape
    blocks = length // LANES
    parts = lax.axis_size("ep")
    place = lax.axis_index("ep")
    share = length // parts
    wide = (rows, length)
    pred = near(predictions)
    leaf = near(leaf_index)
    observed = near(events)
    tie = tie_start.reshape(blocks, LANES)
    later_masks = masks_for("tm", True)
    earlier_masks = masks_for("tm", False)
    starts = jnp.stack([(place ^ d) * share for d in range(parts)]).astype(jnp.int32)

    weight, total = call(weights_body, [resident(wide, F32), resident((rows, LANES), F32)], pred, name="weights")
    _, from_others = across(total, "tm", True)
    risk, last = call(
        risk_body,
        [resident(wide, F32), resident((blocks, LANES), jnp.int32)],
        weight,
        tie,
        scratch=[pltpu.VMEM((blocks, LANES), jnp.int32)],
        name="risk",
    )
    inv, totals = call(
        functools.partial(inverse_body, len(from_others)),
        [resident(wide, F32), resident((2 * rows, LANES), F32)],
        later_masks,
        *from_others,
        risk,
        observed,
        name="inverse",
    )
    _, from_earlier = across(totals, "tm", True)
    local_one, local_two = call(accum_body, [resident(wide, F32)] * 2, inv, last, name="accum")
    *pieces, bases = call(
        functools.partial(pieces_body, len(from_earlier), parts),
        [resident((2, rows, share), BF16)] * parts + [resident((2 * rows, LANES), F32)],
        earlier_masks,
        starts,
        *from_earlier,
        weight,
        observed,
        local_one,
        local_two,
        name="pieces",
    )
    received = [pieces[0]]
    for d in range(1, parts):
        received.append(lax.ppermute(pieces[d], "ep", [(i, i ^ d) for i in range(parts)]))
    (partial_sums,) = call(
        leaf_sums_body,
        [resident((rows, LANES), F32)],
        leaf,
        weight,
        observed,
        local_one,
        local_two,
        bases,
        scratch=[pltpu.VMEM((rows // GROUP, 4 * HIGH * GROUP, LOW * GROUP), F32)],
        name="leaf_sums",
    )
    both, others = across(partial_sums, "tm", True)
    sums = [both] + others[1:]
    while len(sums) > 1:
        sums = [a + b for a, b in zip(sums[::2], sums[1::2])]
    sums = sums[0]
    new_pred, leaf_weights = call(
        update_body,
        [jax.ShapeDtypeStruct(wide, F32), jax.ShapeDtypeStruct((rows, LEAVES), F32)],
        pred,
        leaf,
        sums,
        name="update",
    )
    grad_hess = jnp.zeros((2, rows * parts, 1, share), BF16)
    for d in range(parts):
        grad_hess = lax.dynamic_update_slice(grad_hess, received[d][:, :, None, :], (0, (place ^ d) * rows, 0, 0))
    return new_pred, leaf_weights, grad_hess


def solution(mesh):
    placed = (P("ep", "tm"), P("ep", "tm"), P("ep", "tm"), P("tm"))
    return jax.shard_map(
        on_device,
        mesh=mesh,
        in_specs=placed,
        out_specs=(P("ep", "tm"), P("ep", None), P(None, None, "tm", "ep")),
        check_vma=False,
    )
```

```python
import functools

import jax
import jax.numpy as jnp
from jax import lax
from jax.experimental import pallas as pl
from jax.experimental.pallas import tpu as pltpu
from jax.sharding import PartitionSpec as P

LEAVES = 64
LANES = 128
WIDE = 256
F32 = jnp.float32
BF16 = jnp.bfloat16
I16 = jnp.int16
CODE = 32766.0 / 6.0
MIB = 1024 * 1024


def resident(shape, dtype):
    return pltpu.VMEM(shape, dtype)


def near(array):
    return pltpu.with_memory_space_constraint(array, pltpu.VMEM)


def call(body, outs, *args, scratch=(), name=None, us=1.0, aliases=None, limit=12, hbm=(), hbm_out=()):
    vmem = pl.BlockSpec(memory_space=pltpu.VMEM)
    smem = pl.BlockSpec(memory_space=pltpu.SMEM)
    anywhere = pl.BlockSpec(memory_space=pltpu.HBM)
    return pl.pallas_call(
        body,
        out_shape=outs,
        in_specs=[anywhere if k in hbm else smem if a.ndim == 1 else vmem for k, a in enumerate(args)],
        out_specs=[anywhere if k in hbm_out else vmem for k in range(len(outs))],
        scratch_shapes=list(scratch),
        input_output_aliases=aliases or {},
        compiler_params=pltpu.CompilerParams(vmem_limit_bytes=limit * MIB),
        cost_estimate=pl.CostEstimate(flops=0, bytes_accessed=int(us * 3.5e6), transcendentals=0),
        name=name,
    )(*args)


def lane_sum(x):
    return jnp.broadcast_to(jnp.sum(x, axis=1, keepdims=True), (x.shape[0], LANES))


def fold(x):
    parts = [x[:, k : k + LANES] for k in range(0, x.shape[1], LANES)]
    while len(parts) > 1:
        parts = [a + b for a, b in zip(parts[::2], parts[1::2])] + parts[len(parts) & ~1 :]
    return parts[0]


def span(start, size):
    return pl.ds(pl.multiple_of(start, size), size)


def widen(x, step):
    return jnp.concatenate([x] * (step // LANES), axis=1)


def share_of(meta, d, size):
    return (meta[0] ^ d) * size


def front_body(parts, turns, meta, pred_in, events_in, pred, events, weight, total, *rest):
    messages, sems = rest[: parts - 1], rest[parts - 1]
    rows, length = pred.shape
    width = length // turns

    def copies(turn):
        at = span(turn * width, width)
        return [
            pltpu.make_async_copy(pred_in.at[:, at], pred.at[:, at], sems.at[0, turn]),
            pltpu.make_async_copy(events_in.at[:, at], events.at[:, at], sems.at[1, turn]),
        ]

    for turn in range(turns):
        for copy in copies(turn):
            copy.start()
    step = min(width, 1024)
    acc = jnp.zeros((rows, LANES), F32)
    for turn in range(turns):
        for copy in copies(turn):
            copy.wait()

        def one(k, acc):
            at = span(turn * width + k * step, step)
            value = jnp.exp(pred[:, at])
            weight[:, at] = value
            return acc + fold(value)

        acc = lax.fori_loop(0, width // step, one, acc, unroll=2)
    total[...] = lane_sum(acc)
    share = length // parts
    for d in range(1, parts):

        def code(k, carry):
            source = span(share_of(meta, d, share) + k * step, step)
            at = span(k * step, step)
            messages[d - 1][0, :, at] = jnp.round(pred[:, source] * CODE).astype(jnp.int32).astype(I16)
            messages[d - 1][1, :, at] = events[:, source].astype(I16)
            return carry

        lax.fori_loop(0, share // step, code, 0, unroll=2)


def pair_dot(x, matrix):
    high = x.astype(BF16)
    low = (x - high.astype(F32)).astype(BF16)
    return jnp.dot(high, matrix, preferred_element_type=F32) + jnp.dot(low, matrix, preferred_element_type=F32)


def take(x, index):
    return jnp.take_along_axis(x, index, axis=1, mode="promise_in_bounds")


def last_in_group(starts):
    lane = lax.broadcasted_iota(jnp.int32, starts.shape, 1)
    after = pltpu.roll(starts, LANES - 1, 1)
    best = jnp.where((after == 1) | (lane == LANES - 1), lane, LANES - 1)
    for shift in (1, 2, 4, 8, 16, 32, 64):
        moved = pltpu.roll(best, LANES - shift, 1)
        best = jnp.where(lane < LANES - shift, jnp.minimum(best, moved), best)
    return best


def triangle(backward):
    above = lax.broadcasted_iota(jnp.int32, (WIDE, WIDE), 0)
    along = lax.broadcasted_iota(jnp.int32, (WIDE, WIDE), 1)
    return (above >= along if backward else above <= along).astype(BF16)


def stacked(ref, base, count):
    return jnp.concatenate([ref[:, span(base + k * WIDE, WIDE)] for k in range(count)], axis=0)


def group_events(observed, counts, first, last):
    return jnp.where(first == 1, take(counts, last) - counts + observed, 0.0)


def scan_body(weight, events, tie, leaf_in, suffix, grouped, last, leaf, upper, lower, sem):
    rows, length = weight.shape
    fetch = pltpu.make_async_copy(leaf_in, leaf, sem)
    fetch.start()
    count = min(16, length // WIDE)
    last[...] = last_in_group(tie[...])
    upper[...] = triangle(True)
    lower[...] = triangle(False)
    steps = length // (WIDE * count)

    def one(turn, carry):
        base = (steps - 1 - turn) * (WIDE * count)
        observed = stacked(events, base, count).astype(F32)
        counts = jnp.dot(observed.astype(BF16), lower[...], preferred_element_type=F32)
        summed = pair_dot(stacked(weight, base, count), upper[...])
        for k in range(count - 1, -1, -1):
            mine = slice(k * rows, (k + 1) * rows)
            for half in (0, 1):
                lanes = slice(half * LANES, (half + 1) * LANES)
                at = span(base + k * WIDE + half * LANES, LANES)
                block = pl.ds((base + k * WIDE) // LANES + half, 1)
                suffix[:, at] = summed[mine, lanes] + carry
                grouped[:, at] = group_events(
                    observed[mine, lanes],
                    counts[mine, lanes],
                    jnp.broadcast_to(tie[block, :], (rows, LANES)),
                    jnp.broadcast_to(last[block, :], (rows, LANES)),
                )
            carry = carry + jnp.broadcast_to(summed[mine, 0:1], (rows, LANES))
        return carry

    lax.fori_loop(0, steps, one, jnp.zeros((rows, LANES), F32), unroll=2)
    fetch.wait()


def pair_body(left, right, out):
    out[...] = left[...] + right[...]


def gathered_sum(meta, refs, later):
    mine = meta[1]
    out = None
    for k, ref in enumerate(refs):
        other = mine ^ (1 if k == 0 else 2 * k)
        wanted = (other > mine) if later else (other < mine)
        term = ref[...] * wanted.astype(F32)
        out = term if out is None else out + term
    return out


def inverse_body(count, parts, *refs):
    meta, others = refs[0], refs[1 : 1 + count]
    suffix, grouped, inv_one, inv_two, totals, after = refs[1 + count :]
    rows, length = suffix.shape
    share = length // parts
    later = gathered_sum(meta, others, True)
    for part in range(parts - 1):
        after[part] = jnp.broadcast_to(suffix[:, (part + 1) * share : (part + 1) * share + 1], (rows, LANES)) + later
    after[parts - 1] = later
    step = min(length, 512)

    def one(turn, acc):
        sum_one, sum_two = acc
        at = span(turn * step, step)
        inverse = 1.0 / (suffix[:, at] + widen(later, step))
        first = grouped[:, at] * inverse
        second = first * inverse
        inv_one[:, at] = first
        inv_two[:, at] = second
        return (sum_one + fold(first), sum_two + fold(second))

    empty = jnp.zeros((rows, LANES), F32)
    sum_one, sum_two = lax.fori_loop(0, length // step, one, (empty, empty), unroll=2)
    totals[:rows, :] = lane_sum(sum_one)
    totals[rows:, :] = lane_sum(sum_two)


def accum_body(parts, inv_one, inv_two, one_out, two_out, before, lower):
    rows, length = inv_one.shape
    share = length // parts
    count = min(16, share // WIDE)
    lower[...] = triangle(False)
    empty = jnp.zeros((rows, LANES), F32)
    carry = (empty, empty)
    for part in range(parts):
        before[part, :rows] = carry[0]
        before[part, rows:] = carry[1]

        def one(turn, carry):
            base = part * share + turn * (WIDE * count)
            made = []
            for ref, out, so_far in ((inv_one, one_out, carry[0]), (inv_two, two_out, carry[1])):
                summed = pair_dot(stacked(ref, base, count), lower[...])
                for k in range(count):
                    piece = summed[k * rows : (k + 1) * rows]
                    out[:, span(base + k * WIDE, WIDE)] = piece + widen(so_far, WIDE)
                    so_far = so_far + jnp.broadcast_to(piece[:, WIDE - 1 :], (rows, LANES))
                made.append(so_far)
            return tuple(made)

        carry = lax.fori_loop(0, share // (WIDE * count), one, carry, unroll=2)


def bases_body(count, parts, *refs):
    meta, others = refs[0], refs[1 : 1 + count]
    after, before, bases, *messages = refs[1 + count :]
    rows = after.shape[1]
    earlier = gathered_sum(meta, others, False)
    bases[...] = earlier
    for d in range(1, parts):
        part = share_of(meta, d, 1)
        messages[d - 1][:rows] = after[part]
        messages[d - 1][rows:] = before[part] + earlier


def derivatives(weight, observed, accum_one, accum_two):
    scaled = weight * accum_one
    return scaled - observed, scaled - weight * weight * accum_two


def finish_body(partners, with_own, *refs):
    meta, tie, last = refs[:3]
    refs = refs[3:]
    messages, base = refs[: len(partners)], refs[len(partners) : 2 * len(partners)]
    refs = refs[2 * len(partners) :]
    if with_own:
        weight, events, local_one, local_two, own_bases = refs[:5]
        refs = refs[5:]
    else:
        refs = refs[1:]
    out, scratch, kept, inv_one, inv_two, upper, lower, sems = refs
    _, rows, share = kept.shape
    count = min(8, share // WIDE)
    steps = share // (WIDE * count)
    turn_width = WIDE * count
    first_block = share_of(meta, 0, share) // LANES
    upper[...] = triangle(True)
    lower[...] = triangle(False)
    places = list(partners) + ([0] if with_own else [])
    copies = []
    for slot, d in enumerate(places):
        where = pl.ds(pl.multiple_of(share_of(meta, d, rows), rows), rows)
        copies += [pltpu.make_async_copy(scratch.at[slot, v], out.at[v, where, :], sems.at[slot, v]) for v in (0, 1)]

    if with_own:
        slot = len(partners)
        step = min(share, 512)

        def own(turn, carry):
            source = span(share_of(meta, 0, share) + turn * step, step)
            at = span(turn * step, step)
            grad, hess = derivatives(
                weight[:, source],
                events[:, source].astype(F32),
                local_one[:, source] + widen(own_bases[:rows, :], step),
                local_two[:, source] + widen(own_bases[rows:, :], step),
            )
            scratch[slot, 0, :, at] = grad.astype(BF16)
            scratch[slot, 1, :, at] = hess.astype(BF16)
            return carry

        lax.fori_loop(0, share // step, own, 0, unroll=2)
        for v in (0, 1):
            copies[2 * slot + v].start()

    def one(turn, carry):
        at_base = (steps - 1 - turn) * turn_width
        made = []
        for slot in range(len(partners)):
            coded = jnp.concatenate([messages[slot][0, :, span(at_base + k * WIDE, WIDE)] for k in range(count)], axis=0)
            values = jnp.exp(coded.astype(jnp.int32).astype(F32) * (1.0 / CODE))
            seen = jnp.concatenate([messages[slot][1, :, span(at_base + k * WIDE, WIDE)] for k in range(count)], axis=0)
            observed = seen.astype(jnp.int32).astype(F32)
            counts = jnp.dot(observed.astype(BF16), lower[...], preferred_element_type=F32)
            summed = pair_dot(values, upper[...])
            so_far = carry[slot]
            for k in range(count - 1, -1, -1):
                mine = slice(k * rows, (k + 1) * rows)
                kept[slot, :, span(at_base + k * WIDE, WIDE)] = values[mine]
                for half in (0, 1):
                    lanes = slice(half * LANES, (half + 1) * LANES)
                    at = span(at_base + k * WIDE + half * LANES, LANES)
                    block = pl.ds(first_block + (at_base + k * WIDE) // LANES + half, 1)
                    inverse = 1.0 / (summed[mine, lanes] + so_far)
                    grouped = group_events(
                        observed[mine, lanes],
                        counts[mine, lanes],
                        jnp.broadcast_to(tie[block, :], (rows, LANES)),
                        jnp.broadcast_to(last[block, :], (rows, LANES)),
                    )
                    inv_one[slot, :, at] = grouped * inverse
                    inv_two[slot, :, at] = grouped * inverse * inverse
                so_far = so_far + jnp.broadcast_to(summed[mine, 0:1], (rows, LANES))
            made.append(so_far)
        return tuple(made)

    lax.fori_loop(0, steps, one, tuple(b[:rows, :] for b in base))

    def two(turn, carry):
        at_base = turn * turn_width
        made = []
        for slot in range(len(partners)):
            sum_one = pair_dot(stacked(inv_one.at[slot], at_base, count), lower[...])
            sum_two = pair_dot(stacked(inv_two.at[slot], at_base, count), lower[...])
            so_one, so_two = carry[slot]
            for k in range(count):
                mine = slice(k * rows, (k + 1) * rows)
                at = span(at_base + k * WIDE, WIDE)
                grad, hess = derivatives(
                    kept[slot, :, at],
                    messages[slot][1, :, at].astype(jnp.int32).astype(F32),
                    sum_one[mine] + widen(so_one, WIDE),
                    sum_two[mine] + widen(so_two, WIDE),
                )
                scratch[slot, 0, :, at] = grad.astype(BF16)
                scratch[slot, 1, :, at] = hess.astype(BF16)
                so_one = so_one + jnp.broadcast_to(sum_one[mine, WIDE - 1 :], (rows, LANES))
                so_two = so_two + jnp.broadcast_to(sum_two[mine, WIDE - 1 :], (rows, LANES))
            made.append((so_one, so_two))
        return tuple(made)

    lax.fori_loop(0, steps, two, tuple((b[rows : 2 * rows, :], b[2 * rows :, :]) for b in base))
    for copy in copies[: 2 * len(partners)]:
        copy.start()
    for copy in copies:
        copy.wait()


GROUP = 16
LOW = 16
HIGH = LEAVES // LOW


def leaf_sums_body(leaf, weight, events, local_one, local_two, bases, sums, acc):
    rows, length = weight.shape
    step = min(length, 1024)
    groups = rows // GROUP
    acc[...] = jnp.zeros_like(acc)

    def one(turn, carry):
        at = span(turn * step, step)
        for group in range(groups):
            mine = pl.ds(group * GROUP, GROUP)
            pair = derivatives(
                weight[mine, at],
                events[mine, at].astype(F32),
                local_one[mine, at] + widen(bases[mine, :], step),
                local_two[mine, at] + widen(bases[pl.ds(rows + group * GROUP, GROUP), :], step),
            )
            label = leaf[mine, at]
            low = (label & (LOW - 1)).astype(F32).astype(BF16)
            high = lax.shift_right_logical(label, LOW.bit_length() - 1).astype(F32).astype(BF16)
            terms = []
            for value in pair:
                upper = value.astype(BF16)
                terms += [upper, (value - upper.astype(F32)).astype(BF16)]
            zero = jnp.zeros((GROUP, step), BF16)
            unit = jnp.ones((GROUP, step), BF16)
            left = jnp.concatenate([jnp.where(high == h, term, zero) for term in terms for h in range(HIGH)], axis=0)
            right = jnp.concatenate([jnp.where(low == k, unit, zero) for k in range(LOW)], axis=0)
            acc[group] += lax.dot_general(left, right, (((1,), (1,)), ((), ())), preferred_element_type=F32)
        return carry

    lax.fori_loop(0, length // step, one, 0, unroll=4)
    width = LOW * GROUP
    side = HIGH * GROUP
    same = lax.broadcasted_iota(jnp.int32, (side, width), 0) % GROUP == lax.broadcasted_iota(jnp.int32, (side, width), 1) % GROUP
    source = lax.broadcasted_iota(jnp.int32, (width, LANES), 0) // GROUP
    target = lax.broadcasted_iota(jnp.int32, (width, LANES), 1)
    for group in range(groups):
        out = jnp.zeros((GROUP, LANES), F32)
        for value in (0, 1):
            both = acc[group, 2 * value * side : (2 * value + 1) * side] + acc[group, (2 * value + 1) * side : (2 * value + 2) * side]
            both = jnp.where(same, both, 0.0)
            for h in range(HIGH):
                place = (target == source + (h * LOW + value * LEAVES)).astype(F32)
                out = out + jnp.dot(
                    both[h * GROUP : (h + 1) * GROUP], place, precision=lax.Precision.HIGHEST, preferred_element_type=F32
                )
        sums[group * GROUP : (group + 1) * GROUP, :] = out


def update_body(turns, pred, leaf, *refs):
    sums, (new_pred, leaf_weights, scratch, sems) = refs[:-4], refs[-4:]
    rows, length = pred.shape
    both = [ref[...] for ref in sums]
    while len(both) > 1:
        both = [a + b for a, b in zip(both[::2], both[1::2])]
    table = -both[0] / (pltpu.roll(both[0], LANES - LEAVES, 1) + 1.0)
    leaf_weights[...] = table[:, :LEAVES]
    width = length // turns
    step = min(width, 512)
    copies = []
    for turn in range(turns):

        def one(k, carry):
            at = span(turn * width + k * step, step)
            label = leaf[:, at]
            picked = [take(table, label[:, j : j + LANES]) for j in range(0, step, LANES)]
            scratch[:, at] = pred[:, at] + jnp.concatenate(picked, axis=1)
            return carry

        lax.fori_loop(0, width // step, one, 0, unroll=4)
        at = pl.ds(turn * width, width)
        copies.append(pltpu.make_async_copy(scratch.at[:, at], new_pred.at[:, at], sems.at[turn]))
        copies[-1].start()
    for copy in copies:
        copy.wait()


def swap(array, axis, d):
    return lax.ppermute(array, axis, [(i, i ^ d) for i in range(lax.axis_size(axis))])


def across(total, axis):
    mate = swap(total, axis, 1)
    (both,) = call(pair_body, [resident(total.shape, F32)], total, mate, name="pair", us=0.3, limit=2)
    return both, [mate] + [swap(both, axis, d) for d in range(2, lax.axis_size(axis), 2)]


def on_device(predictions, leaf_index, events, tie_start):
    rows, length = predictions.shape
    blocks = length // LANES
    parts = lax.axis_size("ep")
    share = length // parts
    wide = (rows, length)
    turns = 8
    dma = pltpu.SemaphoreType.DMA
    tie = near(tie_start.reshape(blocks, LANES))
    meta = jnp.stack([lax.axis_index("ep"), lax.axis_index("tm")]).astype(jnp.int32)

    pred, observed, weight, total, *messages = call(
        functools.partial(front_body, parts, turns),
        [resident(wide, F32), resident(wide, jnp.int32), resident(wide, F32), resident((rows, LANES), F32)]
        + [resident((2, rows, share), I16)] * (parts - 1),
        meta,
        predictions,
        events,
        hbm=(1, 2),
        scratch=[dma((2, turns))],
        name="front",
        us=4,
    )
    coded = {d: swap(messages[d - 1], "ep", d) for d in range(parts - 1, 0, -1)}
    _, from_later = across(total, "tm")
    suffix, grouped, last, leaf = call(
        scan_body,
        [resident(wide, F32), resident(wide, F32), resident((blocks, LANES), jnp.int32), resident(wide, jnp.int32)],
        weight,
        observed,
        tie,
        leaf_index,
        hbm=(3,),
        scratch=[pltpu.VMEM((WIDE, WIDE), BF16)] * 2 + [dma],
        name="scan",
        us=5,
    )
    count = len(from_later)
    inv_one, inv_two, totals, after = call(
        functools.partial(inverse_body, count, parts),
        [resident(wide, F32), resident(wide, F32), resident((2 * rows, LANES), F32), resident((parts, rows, LANES), F32)],
        meta,
        *from_later,
        suffix,
        grouped,
        aliases={1 + count: 0, 2 + count: 1},
        name="inverse",
        us=1.5,
    )
    _, from_earlier = across(totals, "tm")
    local_one, local_two, before = call(
        functools.partial(accum_body, parts),
        [resident(wide, F32), resident(wide, F32), resident((parts, 2 * rows, LANES), F32)],
        inv_one,
        inv_two,
        aliases={0: 0, 1: 1},
        scratch=[pltpu.VMEM((WIDE, WIDE), BF16)],
        name="accum",
        us=3,
    )
    bases, *sent = call(
        functools.partial(bases_body, count, parts),
        [resident((2 * rows, LANES), F32)] + [resident((3 * rows, LANES), F32)] * (parts - 1),
        meta,
        *from_earlier,
        after,
        before,
        name="bases",
        us=0.5,
    )
    base = {d: swap(sent[d - 1], "ep", d) for d in range(parts - 1, 0, -1)}
    (partial_sums,) = call(
        leaf_sums_body,
        [resident((rows, LANES), F32)],
        leaf,
        weight,
        observed,
        local_one,
        local_two,
        bases,
        scratch=[pltpu.VMEM((rows // GROUP, 4 * HIGH * GROUP, LOW * GROUP), F32)],
        name="leaf_sums",
        us=10,
    )
    both, others = across(partial_sums, "tm")

    def finish(partners, more, out, name, us):
        held = len(partners) + (out is None)
        args = [meta, tie, last, *[coded[d] for d in partners], *[base[d] for d in partners], *more]
        made = [pltpu.VMEM((len(partners), rows, share), F32)] * 3
        return call(
            functools.partial(finish_body, partners, out is None),
            [jax.ShapeDtypeStruct((2, rows * parts, share), BF16)],
            *args,
            *([] if out is None else [out]),
            hbm=() if out is None else (len(args),),
            hbm_out=(0,),
            aliases=None if out is None else {len(args): 0},
            scratch=[pltpu.VMEM((held, 2, rows, share), BF16), *made, *[pltpu.VMEM((WIDE, WIDE), BF16)] * 2, dma((held, 2))],
            name=name,
            us=us,
        )[0]

    first = parts - 1
    grad_hess = finish([first], [weight, observed, local_one, local_two, bases], None, "finish_first", 5)
    new_pred, leaf_weights = call(
        functools.partial(update_body, turns),
        [jax.ShapeDtypeStruct(wide, F32), jax.ShapeDtypeStruct((rows, LEAVES), F32)],
        pred,
        leaf,
        both,
        *others[1:],
        hbm_out=(0,),
        scratch=[pltpu.VMEM(wide, F32), dma((turns,))],
        name="update",
        us=4,
    )
    grad_hess = finish(list(range(1, first)), [], grad_hess, "finish_rest", 6)
    return new_pred, leaf_weights, grad_hess.reshape(2, rows * parts, 1, share)


def solution(mesh):
    placed = (P("ep", "tm"), P("ep", "tm"), P("ep", "tm"), P("tm"))
    return jax.shard_map(
        on_device,
        mesh=mesh,
        in_specs=placed,
        out_specs=(P("ep", "tm"), P("ep", None), P(None, None, "tm", "ep")),
        check_vma=False,
    )
```

```python
import functools
import math

import jax
import jax.numpy as jnp
from jax import lax
from jax.experimental import pallas as pl
from jax.experimental.pallas import tpu as pltpu
from jax.sharding import PartitionSpec as P

LEAVES = 64
LANES = 128
WIDE = 256
F32 = jnp.float32
BF16 = jnp.bfloat16
I16 = jnp.int16
CODE = 32766.0 / 6.0
MIB = 1024 * 1024


def resident(shape, dtype):
    return pltpu.VMEM(shape, dtype)


def near(array):
    return pltpu.with_memory_space_constraint(array, pltpu.VMEM)


def far(array):
    return pltpu.with_memory_space_constraint(array, pltpu.HBM)


def call(body, outs, *args, scratch=(), name=None, us=1.0, aliases=None, limit=12, hbm=(), hbm_out=()):
    vmem = pl.BlockSpec(memory_space=pltpu.VMEM)
    smem = pl.BlockSpec(memory_space=pltpu.SMEM)
    anywhere = pl.BlockSpec(memory_space=pltpu.HBM)
    return pl.pallas_call(
        body,
        out_shape=outs,
        in_specs=[anywhere if k in hbm else smem if a.ndim == 1 else vmem for k, a in enumerate(args)],
        out_specs=[anywhere if k in hbm_out else vmem for k in range(len(outs))],
        scratch_shapes=list(scratch),
        input_output_aliases=aliases or {},
        compiler_params=pltpu.CompilerParams(vmem_limit_bytes=limit * MIB),
        cost_estimate=pl.CostEstimate(flops=0, bytes_accessed=int(us * 3.5e6), transcendentals=0),
        name=name,
    )(*args)


def lane_sum(x):
    return jnp.broadcast_to(jnp.sum(x, axis=1, keepdims=True), (x.shape[0], LANES))


def fold(x):
    parts = [x[:, k : k + LANES] for k in range(0, x.shape[1], LANES)]
    while len(parts) > 1:
        parts = [a + b for a, b in zip(parts[::2], parts[1::2])] + parts[len(parts) & ~1 :]
    return parts[0]


def span(start, size):
    return pl.ds(pl.multiple_of(start, size), size)


def widen(x, step):
    return jnp.concatenate([x] * (step // LANES), axis=1)


def share_of(meta, d, size):
    return (meta[0] ^ d) * size


def encode(meta, d, pred, events, message):
    share = message.shape[2]
    step = min(share, 1024)

    def one(turn, carry):
        source = span(share_of(meta, d, share) + turn * step, step)
        at = span(turn * step, step)
        message[0, :, at] = jnp.round(pred[:, source] * CODE).astype(jnp.int32).astype(I16)
        message[1, :, at] = events[:, source].astype(I16)
        return carry

    lax.fori_loop(0, share // step, one, 0, unroll=2)


def front_body(partners, turns, meta, pred_in, events_in, events, weight, total, *rest):
    messages, pred, sems = rest[:-2], rest[-2], rest[-1]
    rows, length = pred.shape
    width = length // turns

    def copies(turn):
        at = span(turn * width, width)
        return [
            pltpu.make_async_copy(pred_in.at[:, at], pred.at[:, at], sems.at[0, turn]),
            pltpu.make_async_copy(events_in.at[:, at], events.at[:, at], sems.at[1, turn]),
        ]

    for turn in range(turns):
        for copy in copies(turn):
            copy.start()
    step = min(width, 1024)
    acc = jnp.zeros((rows, LANES), F32)
    for turn in range(turns):
        for copy in copies(turn):
            copy.wait()

        def one(k, acc):
            at = span(turn * width + k * step, step)
            value = jnp.exp(pred[:, at])
            weight[:, at] = value
            return acc + fold(value)

        acc = lax.fori_loop(0, width // step, one, acc, unroll=2)
    total[...] = lane_sum(acc)
    for d, message in zip(partners, messages):
        encode(meta, d, pred, events, message)


def pair_dot(x, matrix):
    high = x.astype(BF16)
    low = (x - high.astype(F32)).astype(BF16)
    return jnp.dot(high, matrix, preferred_element_type=F32) + jnp.dot(low, matrix, preferred_element_type=F32)


def take(x, index):
    return jnp.take_along_axis(x, index, axis=1, mode="promise_in_bounds")


def last_in_group(starts):
    lane = lax.broadcasted_iota(jnp.int32, starts.shape, 1)
    after = pltpu.roll(starts, LANES - 1, 1)
    best = jnp.where((after == 1) | (lane == LANES - 1), lane, LANES - 1)
    for shift in (1, 2, 4, 8, 16, 32, 64):
        moved = pltpu.roll(best, LANES - shift, 1)
        best = jnp.where(lane < LANES - shift, jnp.minimum(best, moved), best)
    return best


def triangle(backward):
    above = lax.broadcasted_iota(jnp.int32, (WIDE, WIDE), 0)
    along = lax.broadcasted_iota(jnp.int32, (WIDE, WIDE), 1)
    return (above >= along if backward else above <= along).astype(BF16)


def stacked(ref, base, count):
    return jnp.concatenate([ref[:, span(base + k * WIDE, WIDE)] for k in range(count)], axis=0)


def group_events(observed, counts, first, last):
    return jnp.where(first == 1, take(counts, last) - counts + observed, 0.0)


def scan_body(weight, events, tie, leaf_in, suffix, grouped, last, leaf, upper, lower, sem):
    rows, length = weight.shape
    fetch = pltpu.make_async_copy(leaf_in, leaf, sem)
    fetch.start()
    count = min(16, length // WIDE)
    last[...] = last_in_group(tie[...])
    upper[...] = triangle(True)
    lower[...] = triangle(False)
    steps = length // (WIDE * count)

    def one(turn, carry):
        base = (steps - 1 - turn) * (WIDE * count)
        observed = stacked(events, base, count).astype(F32)
        counts = jnp.dot(observed.astype(BF16), lower[...], preferred_element_type=F32)
        summed = pair_dot(stacked(weight, base, count), upper[...])
        for k in range(count - 1, -1, -1):
            mine = slice(k * rows, (k + 1) * rows)
            for half in (0, 1):
                lanes = slice(half * LANES, (half + 1) * LANES)
                at = span(base + k * WIDE + half * LANES, LANES)
                block = pl.ds((base + k * WIDE) // LANES + half, 1)
                suffix[:, at] = summed[mine, lanes] + carry
                grouped[:, at] = group_events(
                    observed[mine, lanes],
                    counts[mine, lanes],
                    jnp.broadcast_to(tie[block, :], (rows, LANES)),
                    jnp.broadcast_to(last[block, :], (rows, LANES)),
                )
            carry = carry + jnp.broadcast_to(summed[mine, 0:1], (rows, LANES))
        return carry

    lax.fori_loop(0, steps, one, jnp.zeros((rows, LANES), F32), unroll=2)
    fetch.wait()


def pair_body(left, right, *refs):
    refs[-1][...] = left[...] + right[...]


def join_body(*refs):
    rows = refs[0].shape[0]
    for k, ref in enumerate(refs[:-1]):
        refs[-1][k * rows : (k + 1) * rows, :] = ref[...]


def gathered_sum(meta, refs, later):
    mine = meta[1]
    out = None
    for k, ref in enumerate(refs):
        other = mine ^ (1 if k == 0 else 2 * k)
        wanted = (other > mine) if later else (other < mine)
        term = ref[...] * wanted.astype(F32)
        out = term if out is None else out + term
    return out


def inverse_body(count, parts, *refs):
    meta, others = refs[0], refs[1 : 1 + count]
    suffix, grouped, inv_one, inv_two, totals, after = refs[1 + count :]
    rows, length = suffix.shape
    share = length // parts
    later = gathered_sum(meta, others, True)
    for part in range(parts - 1):
        after[part] = jnp.broadcast_to(suffix[:, (part + 1) * share : (part + 1) * share + 1], (rows, LANES)) + later
    after[parts - 1] = later
    step = min(length, 512)

    def one(turn, acc):
        sum_one, sum_two = acc
        at = span(turn * step, step)
        inverse = 1.0 / (suffix[:, at] + widen(later, step))
        first = grouped[:, at] * inverse
        second = first * inverse
        inv_one[:, at] = first
        inv_two[:, at] = second
        return (sum_one + fold(first), sum_two + fold(second))

    empty = jnp.zeros((rows, LANES), F32)
    sum_one, sum_two = lax.fori_loop(0, length // step, one, (empty, empty), unroll=2)
    totals[:rows, :] = lane_sum(sum_one)
    totals[rows:, :] = lane_sum(sum_two)


def accum_body(parts, inv_one, inv_two, one_out, two_out, before, lower):
    rows, length = inv_one.shape
    share = length // parts
    count = min(16, share // WIDE)
    lower[...] = triangle(False)
    empty = jnp.zeros((rows, LANES), F32)
    carry = (empty, empty)
    for part in range(parts):
        before[part, :rows] = carry[0]
        before[part, rows:] = carry[1]

        def one(turn, carry):
            base = part * share + turn * (WIDE * count)
            made = []
            for ref, out, so_far in ((inv_one, one_out, carry[0]), (inv_two, two_out, carry[1])):
                summed = pair_dot(stacked(ref, base, count), lower[...])
                for k in range(count):
                    piece = summed[k * rows : (k + 1) * rows]
                    out[:, span(base + k * WIDE, WIDE)] = piece + widen(so_far, WIDE)
                    so_far = so_far + jnp.broadcast_to(piece[:, WIDE - 1 :], (rows, LANES))
                made.append(so_far)
            return tuple(made)

        carry = lax.fori_loop(0, share // (WIDE * count), one, carry, unroll=2)


def derivatives(weight, observed, accum_one, accum_two):
    scaled = weight * accum_one
    return scaled - observed, scaled - weight * weight * accum_two


def pieces(first, at_rows, weight, events, local_one, local_two, bases, out, at_lanes=0):
    rows, length = out.shape[1], at_rows
    step = math.gcd(length, 512)

    def one(turn, carry):
        source = span(first + turn * step, step)
        at = span(at_lanes + turn * step, step)
        grad, hess = derivatives(
            weight[:, source],
            events[:, source].astype(F32),
            local_one[:, source] + widen(bases[:rows, :], step),
            local_two[:, source] + widen(bases[rows:, :], step),
        )
        out[0, :, at] = grad.astype(BF16)
        out[1, :, at] = hess.astype(BF16)
        return carry

    lax.fori_loop(0, length // step, one, 0, unroll=2)


def bases_body(count, links, diagonals, share, *refs):
    meta, others = refs[0], refs[1 : 1 + count]
    after, before, *scans = refs[1 + count : 7 + count]
    bases, *messages = refs[len(refs) - 1 - len(links) - len(diagonals) :]
    messages, early = messages[: len(links)], messages[len(links) :]
    rows = after.shape[1]
    earlier = gathered_sum(meta, others, False)
    bases[...] = earlier
    for d, message in zip(links, messages):
        part = share_of(meta, d, 1)
        message[:rows] = after[part]
        message[rows:] = before[part] + earlier
    for d, out in zip(diagonals, early):
        pieces(share_of(meta, d, share), out.shape[2], *scans, bases, out)


def rest_body(diagonals, share, meta, *refs):
    for d, out in zip(diagonals, refs[len(refs) - len(diagonals) :]):
        size = out.shape[2]
        pieces(share_of(meta, d, share) + share - size, size, *refs[:5], out)


def place_pieces(meta, partners, arrived, out, sems, last=False):
    copies = []
    for k, (d, piece) in enumerate(zip(partners, arrived)):
        _, rows, size = piece.shape
        where = pl.ds(pl.multiple_of(share_of(meta, d, rows), rows), rows)
        lanes = pl.ds(out.shape[2] - size if last else 0, size)
        copies += [pltpu.make_async_copy(piece.at[v], out.at[v, where, lanes], sems.at[k, v]) for v in (0, 1)]
    return copies


def finish_body(partners, *refs):
    meta, tie, last = refs[:3]
    refs = refs[3:]
    messages, base = refs[: len(partners)], refs[len(partners) : 2 * len(partners)]
    refs = refs[2 * len(partners) :]
    weight, events, local_one, local_two, own_bases = refs[:5]
    pred_in, out, pred, scratch, kept, inv_one, inv_two, upper, lower, sems, fetch_sem = refs[5:]
    fetch = pltpu.make_async_copy(pred_in, pred, fetch_sem)
    fetch.start()
    _, rows, share = kept.shape
    count = min(8, share // WIDE)
    steps = share // (WIDE * count)
    turn_width = WIDE * count
    first_block = share_of(meta, 0, share) // LANES
    upper[...] = triangle(True)
    lower[...] = triangle(False)
    places = list(partners) + [0]
    copies = place_pieces(meta, places, [scratch.at[slot] for slot in range(len(places))], out, sems)
    slot = len(partners)
    pieces(share_of(meta, 0, share), share, weight, events, local_one, local_two, own_bases, scratch.at[slot])
    for v in (0, 1):
        copies[2 * slot + v].start()

    def one(turn, carry):
        at_base = (steps - 1 - turn) * turn_width
        made = []
        for slot in range(len(partners)):
            coded = jnp.concatenate([messages[slot][0, :, span(at_base + k * WIDE, WIDE)] for k in range(count)], axis=0)
            values = jnp.exp(coded.astype(jnp.int32).astype(F32) * (1.0 / CODE))
            seen = jnp.concatenate([messages[slot][1, :, span(at_base + k * WIDE, WIDE)] for k in range(count)], axis=0)
            observed = seen.astype(jnp.int32).astype(F32)
            counts = jnp.dot(observed.astype(BF16), lower[...], preferred_element_type=F32)
            summed = pair_dot(values, upper[...])
            so_far = carry[slot]
            for k in range(count - 1, -1, -1):
                mine = slice(k * rows, (k + 1) * rows)
                kept[slot, :, span(at_base + k * WIDE, WIDE)] = values[mine]
                for half in (0, 1):
                    lanes = slice(half * LANES, (half + 1) * LANES)
                    at = span(at_base + k * WIDE + half * LANES, LANES)
                    block = pl.ds(first_block + (at_base + k * WIDE) // LANES + half, 1)
                    inverse = 1.0 / (summed[mine, lanes] + so_far)
                    grouped = group_events(
                        observed[mine, lanes],
                        counts[mine, lanes],
                        jnp.broadcast_to(tie[block, :], (rows, LANES)),
                        jnp.broadcast_to(last[block, :], (rows, LANES)),
                    )
                    inv_one[slot, :, at] = grouped * inverse
                    inv_two[slot, :, at] = grouped * inverse * inverse
                so_far = so_far + jnp.broadcast_to(summed[mine, 0:1], (rows, LANES))
            made.append(so_far)
        return tuple(made)

    lax.fori_loop(0, steps, one, tuple(b[:rows, :] for b in base))

    def two(turn, carry):
        at_base = turn * turn_width
        made = []
        for slot in range(len(partners)):
            sum_one = pair_dot(stacked(inv_one.at[slot], at_base, count), lower[...])
            sum_two = pair_dot(stacked(inv_two.at[slot], at_base, count), lower[...])
            so_one, so_two = carry[slot]
            for k in range(count):
                mine = slice(k * rows, (k + 1) * rows)
                at = span(at_base + k * WIDE, WIDE)
                grad, hess = derivatives(
                    kept[slot, :, at],
                    messages[slot][1, :, at].astype(jnp.int32).astype(F32),
                    sum_one[mine] + widen(so_one, WIDE),
                    sum_two[mine] + widen(so_two, WIDE),
                )
                scratch[slot, 0, :, at] = grad.astype(BF16)
                scratch[slot, 1, :, at] = hess.astype(BF16)
                so_one = so_one + jnp.broadcast_to(sum_one[mine, WIDE - 1 :], (rows, LANES))
                so_two = so_two + jnp.broadcast_to(sum_two[mine, WIDE - 1 :], (rows, LANES))
            made.append((so_one, so_two))
        return tuple(made)

    lax.fori_loop(0, steps, two, tuple((b[rows : 2 * rows, :], b[2 * rows :, :]) for b in base))
    for copy in copies[: 2 * len(partners)]:
        copy.start()
    for copy in copies:
        copy.wait()
    fetch.wait()


GROUP = 16
LOW = 16
HIGH = LEAVES // LOW


def leaf_sums_body(group, leaf, weight, events, local_one, local_two, bases, *rest):
    sums, acc = rest[-2:]
    rows, length = weight.shape
    step = min(length, 2048)
    mine = pl.ds(group * GROUP, GROUP)
    acc[...] = jnp.zeros_like(acc)

    def one(turn, carry):
        at = span(turn * step, step)
        pair = derivatives(
            weight[mine, at],
            events[mine, at].astype(F32),
            local_one[mine, at] + widen(bases[mine, :], step),
            local_two[mine, at] + widen(bases[pl.ds(rows + group * GROUP, GROUP), :], step),
        )
        label = leaf[mine, at]
        low = (label & (LOW - 1)).astype(F32).astype(BF16)
        high = lax.shift_right_logical(label, LOW.bit_length() - 1).astype(F32).astype(BF16)
        terms = []
        for value in pair:
            upper = value.astype(BF16)
            terms += [upper, (value - upper.astype(F32)).astype(BF16)]
        zero = jnp.zeros((GROUP, step), BF16)
        unit = jnp.ones((GROUP, step), BF16)
        left = jnp.concatenate([jnp.where(high == h, term, zero) for term in terms for h in range(HIGH)], axis=0)
        right = jnp.concatenate([jnp.where(low == k, unit, zero) for k in range(LOW)], axis=0)
        acc[...] += lax.dot_general(left, right, (((1,), (1,)), ((), ())), preferred_element_type=F32)
        return carry

    lax.fori_loop(0, length // step, one, 0, unroll=4)
    width = LOW * GROUP
    side = HIGH * GROUP
    same = lax.broadcasted_iota(jnp.int32, (side, width), 0) % GROUP == lax.broadcasted_iota(jnp.int32, (side, width), 1) % GROUP
    source = lax.broadcasted_iota(jnp.int32, (width, LANES), 0) // GROUP
    target = lax.broadcasted_iota(jnp.int32, (width, LANES), 1)
    out = jnp.zeros((GROUP, LANES), F32)
    for value in (0, 1):
        both = acc[2 * value * side : (2 * value + 1) * side] + acc[(2 * value + 1) * side : (2 * value + 2) * side]
        both = jnp.where(same, both, 0.0)
        for h in range(HIGH):
            place = (target == source + (h * LOW + value * LEAVES)).astype(F32)
            out = out + jnp.dot(both[h * GROUP : (h + 1) * GROUP], place, precision=lax.Precision.HIGHEST, preferred_element_type=F32)
    sums[...] = out


def update_body(turns, partners, meta, pred, leaf, *refs):
    early, late, refs = refs[: len(partners)], refs[len(partners) : 2 * len(partners)], refs[2 * len(partners) + 1 :]
    sums, (new_pred, leaf_weights, out, scratch, sems, early_sems, late_sems) = refs[:-7], refs[-7:]
    rows, length = leaf.shape
    copies = place_pieces(meta, partners, early, out, early_sems)
    copies += place_pieces(meta, partners, late, out, late_sems, True)
    for copy in copies:
        copy.start()
    both = [ref[...] for ref in sums]
    while len(both) > 1:
        both = [a + b for a, b in zip(both[::2], both[1::2])]
    table = -both[0] / (pltpu.roll(both[0], LANES - LEAVES, 1) + 1.0)
    leaf_weights[...] = table[:, :LEAVES]
    width = length // turns
    step = min(width, 512)
    for turn in range(turns):

        def one(k, carry):
            at = span(turn * width + k * step, step)
            label = leaf[:, at]
            picked = [take(table, label[:, j : j + LANES]) for j in range(0, step, LANES)]
            scratch[:, at] = pred[:, at] + jnp.concatenate(picked, axis=1)
            return carry

        lax.fori_loop(0, width // step, one, 0, unroll=8)
        at = pl.ds(turn * width, width)
        copies.append(pltpu.make_async_copy(scratch.at[:, at], new_pred.at[:, at], sems.at[turn]))
        copies[-1].start()
    for copy in copies:
        copy.wait()


def swap(array, axis, d):
    return lax.ppermute(array, axis, [(i, i ^ d) for i in range(lax.axis_size(axis))])


def across(total, axis, arrived=()):
    mate = swap(total, axis, 1)
    (both,) = call(pair_body, [resident(total.shape, F32)], total, mate, *arrived, name="pair", us=0.3, limit=4)
    return both, [mate] + [swap(both, axis, d) for d in range(2, lax.axis_size(axis), 2)]


def on_device(predictions, leaf_index, events, tie_start):
    rows, length = predictions.shape
    blocks = length // LANES
    parts = lax.axis_size("ep")
    share = length // parts
    wide = (rows, length)
    turns = 8
    dma = pltpu.SemaphoreType.DMA
    tie = near(tie_start.reshape(blocks, LANES))
    meta = jnp.stack([lax.axis_index("ep"), lax.axis_index("tm")]).astype(jnp.int32)

    links = [d for d in range(1, parts) if d & (d - 1) == 0]
    diagonals = [d for d in range(1, parts) if d not in links]
    message = resident((2, rows, share), I16)
    observed, weight, total, *messages = call(
        functools.partial(front_body, links, turns),
        [resident(wide, jnp.int32), resident(wide, F32), resident((rows, LANES), F32)] + [message] * len(links),
        meta,
        far(predictions),
        far(events),
        hbm=(1, 2),
        scratch=[pltpu.VMEM(wide, F32), dma((2, turns))],
        name="front",
        us=4,
    )
    coded = {d: swap(m, "ep", d) for d, m in zip(links, messages)}
    _, from_later = across(total, "tm")
    suffix, grouped, last, leaf = call(
        scan_body,
        [resident(wide, F32), resident(wide, F32), resident((blocks, LANES), jnp.int32), resident(wide, jnp.int32)],
        weight,
        observed,
        tie,
        far(leaf_index),
        hbm=(3,),
        scratch=[pltpu.VMEM((WIDE, WIDE), BF16)] * 2 + [dma],
        name="scan",
        us=5,
    )
    count = len(from_later)
    inv_one, inv_two, totals, after = call(
        functools.partial(inverse_body, count, parts),
        [resident(wide, F32), resident(wide, F32), resident((2 * rows, LANES), F32), resident((parts, rows, LANES), F32)],
        meta,
        *from_later,
        suffix,
        grouped,
        aliases={1 + count: 0, 2 + count: 1},
        name="inverse",
        us=1.5,
    )
    _, from_earlier = across(totals, "tm")
    local_one, local_two, before = call(
        functools.partial(accum_body, parts),
        [resident(wide, F32), resident(wide, F32), resident((parts, 2 * rows, LANES), F32)],
        inv_one,
        inv_two,
        aliases={0: 0, 1: 1},
        scratch=[pltpu.VMEM((WIDE, WIDE), BF16)],
        name="accum",
        us=3,
    )
    scans = (weight, observed, local_one, local_two)
    early_rows = share // 4
    bases, *sent = call(
        functools.partial(bases_body, count, links, diagonals, share),
        [resident((2 * rows, LANES), F32)]
        + [resident((3 * rows, LANES), F32)] * len(links)
        + [resident((2, rows, early_rows), BF16)] * len(diagonals),
        meta,
        *from_earlier,
        after,
        before,
        *scans,
        *coded.values(),
        name="bases",
        us=1,
    )
    base = {d: swap(m, "ep", d) for d, m in zip(links, sent)}
    early = [swap(m, "ep", d) for d, m in zip(diagonals, sent[len(links) :])]
    late = []
    partial_sums = []
    for group in range(rows // GROUP):
        partial_sums += call(
            functools.partial(leaf_sums_body, group),
            [resident((GROUP, LANES), F32)],
            leaf,
            *scans,
            bases,
            *(sent if late else []),
            scratch=[pltpu.VMEM((4 * HIGH * GROUP, LOW * GROUP), F32)],
            name="leaf_sums",
            us=5,
        )
        if not late:
            sent = call(
                functools.partial(rest_body, diagonals, share),
                [resident((2, rows, share - early_rows), BF16)] * len(diagonals),
                meta,
                *scans,
                bases,
                *partial_sums,
                *base.values(),
                *early,
                name="rest",
                us=1,
            )
            late = [swap(m, "ep", d) for d, m in zip(diagonals, sent)]
    (own_sums,) = call(join_body, [resident((rows, LANES), F32)], *partial_sums, name="join", us=0.3, limit=2)
    both, others = across(own_sums, "tm", base.values())
    piece = pltpu.VMEM((len(links), rows, share), F32)
    args = [meta, tie, last, *[coded[d] for d in links], *[base[d] for d in links], *scans, bases]
    grad_hess, pred = call(
        functools.partial(finish_body, links),
        [jax.ShapeDtypeStruct((2, rows * parts, share), BF16), resident(wide, F32)],
        *args,
        far(predictions),
        hbm=(len(args),),
        hbm_out=(0,),
        scratch=[pltpu.VMEM((len(links) + 1, 2, rows, share), BF16)]
        + [piece] * 3
        + [pltpu.VMEM((WIDE, WIDE), BF16)] * 2
        + [dma((len(links) + 1, 2)), dma],
        name="finish",
        us=8,
        limit=14,
    )
    at_out = 3 + 2 * len(diagonals)
    new_pred, leaf_weights, grad_hess = call(
        functools.partial(update_body, turns, diagonals),
        [jax.ShapeDtypeStruct(wide, F32), jax.ShapeDtypeStruct((rows, LEAVES), F32), jax.ShapeDtypeStruct(grad_hess.shape, BF16)],
        meta,
        pred,
        leaf,
        *early,
        *late,
        grad_hess,
        both,
        *others[1:],
        hbm=range(3, at_out + 1),
        hbm_out=(0, 2),
        aliases={at_out: 2},
        scratch=[pltpu.VMEM(wide, F32), dma((turns,)), dma((max(1, len(diagonals)), 2)), dma((max(1, len(diagonals)), 2))],
        name="update",
        us=4,
    )
    return new_pred, leaf_weights, grad_hess.reshape(2, rows * parts, 1, share)


def solution(mesh):
    placed = (P("ep", "tm"), P("ep", "tm"), P("ep", "tm"), P("tm"))
    return jax.shard_map(
        on_device,
        mesh=mesh,
        in_specs=placed,
        out_specs=(P("ep", "tm"), P("ep", None), P(None, None, "tm", "ep")),
        check_vma=False,
    )
```

```python
import functools
import math

import jax
import jax.numpy as jnp
from jax import lax
from jax.experimental import pallas as pl
from jax.experimental.pallas import tpu as pltpu
from jax.sharding import PartitionSpec as P

LEAVES = 64
LANES = 128
WIDE = 256
F32 = jnp.float32
BF16 = jnp.bfloat16
I16 = jnp.int16
CODE = 32766.0 / 6.0
MIDDLE = 32768
MIB = 1024 * 1024


def resident(shape, dtype):
    return pltpu.VMEM(shape, dtype)


def near(array):
    return pltpu.with_memory_space_constraint(array, pltpu.VMEM)


def far(array):
    return pltpu.with_memory_space_constraint(array, pltpu.HBM)


def call(body, outs, *args, scratch=(), name=None, us=1.0, aliases=None, limit=12, hbm=(), hbm_out=()):
    vmem = pl.BlockSpec(memory_space=pltpu.VMEM)
    smem = pl.BlockSpec(memory_space=pltpu.SMEM)
    anywhere = pl.BlockSpec(memory_space=pltpu.HBM)
    return pl.pallas_call(
        body,
        out_shape=outs,
        in_specs=[anywhere if k in hbm else smem if a.ndim == 1 else vmem for k, a in enumerate(args)],
        out_specs=[anywhere if k in hbm_out else vmem for k in range(len(outs))],
        scratch_shapes=list(scratch),
        input_output_aliases=aliases or {},
        compiler_params=pltpu.CompilerParams(vmem_limit_bytes=limit * MIB),
        cost_estimate=pl.CostEstimate(flops=0, bytes_accessed=int(us * 3.5e6), transcendentals=0),
        name=name,
    )(*args)


def lane_sum(x):
    return jnp.broadcast_to(jnp.sum(x, axis=1, keepdims=True), (x.shape[0], LANES))


def fold(x):
    parts = [x[:, k : k + LANES] for k in range(0, x.shape[1], LANES)]
    while len(parts) > 1:
        parts = [a + b for a, b in zip(parts[::2], parts[1::2])] + parts[len(parts) & ~1 :]
    return parts[0]


def span(start, size):
    return pl.ds(pl.multiple_of(start, size), size)


def widen(x, step):
    return jnp.concatenate([x] * (step // LANES), axis=1)


def share_of(meta, d, size):
    return (meta[0] ^ d) * size


def encode(meta, d, pred, events, message):
    share = message.shape[2]
    step = min(share, 1024)

    def one(turn, carry):
        source = span(share_of(meta, d, share) + turn * step, step)
        at = span(turn * step, step)
        above = (pred[:, source] * CODE + (MIDDLE + 0.5)).astype(jnp.int32)
        message[0, :, at] = (above - MIDDLE).astype(I16)
        message[1, :, at] = events[:, source].astype(I16)
        return carry

    lax.fori_loop(0, share // step, one, 0, unroll=2)


def front_body(partners, turns, parts, meta, pred_in, events_in, events, weight, total, *rest):
    messages, pred, sems, share_sems = rest[:-3], rest[-3], rest[-2], rest[-1]
    rows, length = pred.shape
    width = length // turns
    share = length // parts
    loads = []
    for turn in range(turns):
        at = span(turn * width, width)
        loads.append(pltpu.make_async_copy(pred_in.at[:, at], pred.at[:, at], sems.at[turn]))
    order = list(partners) + [d for d in range(parts) if d not in partners]
    fetches = []
    for k, d in enumerate(order):
        at = span(share_of(meta, d, share), share)
        fetches.append(pltpu.make_async_copy(events_in.at[:, at], events.at[:, at], share_sems.at[k]))
    for copy in loads + fetches:
        copy.start()
    step = min(width, 1024)
    acc = jnp.zeros((rows, LANES), F32)
    for turn in range(turns):
        loads[turn].wait()

        def one(k, acc):
            at = span(turn * width + k * step, step)
            value = jnp.exp(pred[:, at])
            weight[:, at] = value
            return acc + fold(value)

        acc = lax.fori_loop(0, width // step, one, acc, unroll=2)
    total[...] = lane_sum(acc)
    for k, (d, message) in enumerate(zip(partners, messages)):
        fetches[k].wait()
        encode(meta, d, pred, events, message)
    for copy in fetches[len(partners) :]:
        copy.wait()


def pair_dot(x, matrix):
    high = x.astype(BF16)
    low = (x - high.astype(F32)).astype(BF16)
    return jnp.dot(high, matrix, preferred_element_type=F32) + jnp.dot(low, matrix, preferred_element_type=F32)


def take(x, index):
    return jnp.take_along_axis(x, index, axis=1, mode="promise_in_bounds")


def last_in_group(starts):
    lane = lax.broadcasted_iota(jnp.int32, starts.shape, 1)
    after = pltpu.roll(starts, LANES - 1, 1)
    best = jnp.where((after == 1) | (lane == LANES - 1), lane, LANES - 1)
    for shift in (1, 2, 4, 8, 16, 32, 64):
        moved = pltpu.roll(best, LANES - shift, 1)
        best = jnp.where(lane < LANES - shift, jnp.minimum(best, moved), best)
    return best


def triangle(backward):
    above = lax.broadcasted_iota(jnp.int32, (WIDE, WIDE), 0)
    along = lax.broadcasted_iota(jnp.int32, (WIDE, WIDE), 1)
    return (above >= along if backward else above <= along).astype(BF16)


def stacked(ref, base, count):
    return jnp.concatenate([ref[:, span(base + k * WIDE, WIDE)] for k in range(count)], axis=0)


FIELDS = 4
BITS = 8


def pack(x):
    size = x.shape[0] // FIELDS
    out = x[:size]
    for k in range(1, FIELDS):
        out = out + lax.shift_left(x[k * size : (k + 1) * size], BITS * k)
    return out


def unpack(x):
    return jnp.concatenate([(lax.shift_right_logical(x, BITS * k) & 255).astype(F32) for k in range(FIELDS)], axis=0)


def group_events(observed, counts, first, last):
    held = pack(counts.astype(jnp.int32))
    return jnp.where(first == 1, take(held, last) - held + pack(observed), 0)


def scan_body(weight, events, tie, leaf_in, suffix, grouped, last, leaf, upper, lower, sem):
    rows, length = weight.shape
    fetch = pltpu.make_async_copy(leaf_in, leaf, sem)
    fetch.start()
    count = min(16, length // WIDE)
    last[...] = last_in_group(tie[...])
    upper[...] = triangle(True)
    lower[...] = triangle(False)
    steps = length // (WIDE * count)

    def one(turn, carry):
        base = (steps - 1 - turn) * (WIDE * count)
        observed = stacked(events, base, count)
        counts = jnp.dot(observed.astype(F32).astype(BF16), lower[...], preferred_element_type=F32)
        summed = pair_dot(stacked(weight, base, count), upper[...])
        for k in range(count - 1, -1, -1):
            mine = slice(k * rows, (k + 1) * rows)
            for half in (0, 1):
                lanes = slice(half * LANES, (half + 1) * LANES)
                at = span(base + k * WIDE + half * LANES, LANES)
                block = pl.ds((base + k * WIDE) // LANES + half, 1)
                suffix[:, at] = summed[mine, lanes] + carry
                grouped[:, at] = group_events(
                    observed[mine, lanes],
                    counts[mine, lanes],
                    jnp.broadcast_to(tie[block, :], (rows // FIELDS, LANES)),
                    jnp.broadcast_to(last[block, :], (rows // FIELDS, LANES)),
                )
            carry = carry + jnp.broadcast_to(summed[mine, 0:1], (rows, LANES))
        return carry

    lax.fori_loop(0, steps, one, jnp.zeros((rows, LANES), F32), unroll=2)
    fetch.wait()


def pair_body(left, right, *refs):
    refs[-1][...] = left[...] + right[...]


def gathered_sum(meta, refs, later):
    mine = meta[1]
    out = None
    for k, ref in enumerate(refs):
        other = mine ^ (1 if k == 0 else 2 * k)
        wanted = (other > mine) if later else (other < mine)
        term = ref[...] * wanted.astype(F32)
        out = term if out is None else out + term
    return out


def inverse_body(count, parts, *refs):
    meta, others = refs[0], refs[1 : 1 + count]
    suffix, grouped, inv_one, inv_two, totals, after = refs[1 + count :]
    rows, length = suffix.shape
    share = length // parts
    later = gathered_sum(meta, others, True)
    for part in range(parts - 1):
        after[part] = jnp.broadcast_to(suffix[:, (part + 1) * share : (part + 1) * share + 1], (rows, LANES)) + later
    after[parts - 1] = later
    step = min(length, 512)

    def one(turn, acc):
        sum_one, sum_two = acc
        at = span(turn * step, step)
        inverse = 1.0 / (suffix[:, at] + widen(later, step))
        first = unpack(grouped[:, at]) * inverse
        second = first * inverse
        inv_one[:, at] = first
        inv_two[:, at] = second
        return (sum_one + fold(first), sum_two + fold(second))

    empty = jnp.zeros((rows, LANES), F32)
    sum_one, sum_two = lax.fori_loop(0, length // step, one, (empty, empty), unroll=2)
    totals[:rows, :] = lane_sum(sum_one)
    totals[rows:, :] = lane_sum(sum_two)


def accum_body(parts, inv_one, inv_two, one_out, two_out, before, lower):
    rows, length = inv_one.shape
    share = length // parts
    count = min(16, share // WIDE)
    lower[...] = triangle(False)
    empty = jnp.zeros((rows, LANES), F32)
    carry = (empty, empty)
    for part in range(parts):
        before[part, :rows] = carry[0]
        before[part, rows:] = carry[1]

        def one(turn, carry):
            base = part * share + turn * (WIDE * count)
            made = []
            for ref, out, so_far in ((inv_one, one_out, carry[0]), (inv_two, two_out, carry[1])):
                summed = pair_dot(stacked(ref, base, count), lower[...])
                for k in range(count):
                    piece = summed[k * rows : (k + 1) * rows]
                    out[:, span(base + k * WIDE, WIDE)] = piece + widen(so_far, WIDE)
                    so_far = so_far + jnp.broadcast_to(piece[:, WIDE - 1 :], (rows, LANES))
                made.append(so_far)
            return tuple(made)

        carry = lax.fori_loop(0, share // (WIDE * count), one, carry, unroll=2)


def derivatives(weight, observed, accum_one, accum_two):
    scaled = weight * accum_one
    return scaled - observed, scaled - weight * weight * accum_two


def bases_body(count, links, *refs):
    meta, others = refs[0], refs[1 : 1 + count]
    after, before = refs[1 + count : 3 + count]
    bases, *messages = refs[len(refs) - 1 - len(links) :]
    rows = after.shape[1]
    earlier = gathered_sum(meta, others, False)
    bases[...] = earlier
    for d, message in zip(links, messages):
        part = share_of(meta, d, 1)
        message[:rows] = after[part]
        message[rows:] = before[part] + earlier


def release_body(*refs):
    pass


def place_pieces(meta, partners, arrived, out, sems):
    copies = []
    for k, (d, piece) in enumerate(zip(partners, arrived)):
        rows = piece.shape[1]
        where = pl.ds(pl.multiple_of(share_of(meta, d, rows), rows), rows)
        copies += [pltpu.make_async_copy(piece.at[v], out.at[v, where, :], sems.at[k, v]) for v in (0, 1)]
    return copies


def finish_body(partners, *refs):
    meta, tie, last = refs[:3]
    refs = refs[3:]
    messages, base = refs[: len(partners)], refs[len(partners) : 2 * len(partners)]
    own, pred_in, out, pred, scratch, kept, inv_one, inv_two, upper, lower, sems, own_sems, fetch_sem = refs[2 * len(partners) :]
    fetch = pltpu.make_async_copy(pred_in, pred, fetch_sem)
    fetch.start()
    own_copies = place_pieces(meta, [0], [own], out, own_sems)
    for copy in own_copies:
        copy.start()
    _, rows, share = kept.shape
    count = share // (WIDE * sems.shape[2])
    steps = share // (WIDE * count)
    turn_width = WIDE * count
    first_block = share_of(meta, 0, share) // LANES
    upper[...] = triangle(True)
    lower[...] = triangle(False)

    def one(turn, carry):
        at_base = (steps - 1 - turn) * turn_width
        made = []
        for slot in range(len(partners)):
            coded = jnp.concatenate([messages[slot][0, :, span(at_base + k * WIDE, WIDE)] for k in range(count)], axis=0)
            values = jnp.exp(coded.astype(jnp.int32).astype(F32) * (1.0 / CODE))
            seen = jnp.concatenate([messages[slot][1, :, span(at_base + k * WIDE, WIDE)] for k in range(count)], axis=0)
            observed = seen.astype(jnp.int32)
            counts = jnp.dot(observed.astype(F32).astype(BF16), lower[...], preferred_element_type=F32)
            summed = pair_dot(values, upper[...])
            so_far = carry[slot]
            for k in range(count - 1, -1, -1):
                mine = slice(k * rows, (k + 1) * rows)
                kept[slot, :, span(at_base + k * WIDE, WIDE)] = values[mine]
                for half in (0, 1):
                    lanes = slice(half * LANES, (half + 1) * LANES)
                    at = span(at_base + k * WIDE + half * LANES, LANES)
                    block = pl.ds(first_block + (at_base + k * WIDE) // LANES + half, 1)
                    grouped = group_events(
                        observed[mine, lanes],
                        counts[mine, lanes],
                        jnp.broadcast_to(tie[block, :], (rows // FIELDS, LANES)),
                        jnp.broadcast_to(last[block, :], (rows // FIELDS, LANES)),
                    )
                    inverse = 1.0 / (summed[mine, lanes] + so_far)
                    first = unpack(grouped) * inverse
                    inv_one[slot, :, at] = first
                    inv_two[slot, :, at] = first * inverse
                so_far = so_far + jnp.broadcast_to(summed[mine, 0:1], (rows, LANES))
            made.append(so_far)
        return tuple(made)

    lax.fori_loop(0, steps, one, tuple(b[:rows, :] for b in base))

    def copies(turn):
        lanes = span(turn * turn_width, turn_width)
        made = []
        for slot, d in enumerate(partners):
            where = pl.ds(pl.multiple_of(share_of(meta, d, rows), rows), rows)
            made += [
                pltpu.make_async_copy(scratch.at[slot, v, :, lanes], out.at[v, where, lanes], sems.at[slot, v, turn])
                for v in (0, 1)
            ]
        return made

    def two(turn, carry):
        at_base = turn * turn_width
        made = []
        for slot in range(len(partners)):
            sum_one = pair_dot(stacked(inv_one.at[slot], at_base, count), lower[...])
            sum_two = pair_dot(stacked(inv_two.at[slot], at_base, count), lower[...])
            so_one, so_two = carry[slot]
            for k in range(count):
                mine = slice(k * rows, (k + 1) * rows)
                at = span(at_base + k * WIDE, WIDE)
                grad, hess = derivatives(
                    kept[slot, :, at],
                    messages[slot][1, :, at].astype(jnp.int32).astype(F32),
                    sum_one[mine] + widen(so_one, WIDE),
                    sum_two[mine] + widen(so_two, WIDE),
                )
                scratch[slot, 0, :, at] = grad.astype(BF16)
                scratch[slot, 1, :, at] = hess.astype(BF16)
                so_one = so_one + jnp.broadcast_to(sum_one[mine, WIDE - 1 :], (rows, LANES))
                so_two = so_two + jnp.broadcast_to(sum_two[mine, WIDE - 1 :], (rows, LANES))
            made.append((so_one, so_two))
        for copy in copies(turn):
            copy.start()
        return tuple(made)

    lax.fori_loop(0, steps, two, tuple((b[rows : 2 * rows, :], b[2 * rows :, :]) for b in base))
    for turn in range(steps):
        for copy in copies(turn):
            copy.wait()
    for copy in own_copies:
        copy.wait()
    fetch.wait()


GROUP = 16
LOW = 16
HIGH = LEAVES // LOW


def leaf_step(at, leaf, weight, events, local_one, local_two, bases, acc, out, at_out):
    rows = weight.shape[0]
    step = at.size
    zero = jnp.zeros((GROUP, step), BF16)
    unit = jnp.ones((GROUP, step), BF16)
    for group in range(rows // GROUP):
        mine = pl.ds(group * GROUP, GROUP)
        pair = derivatives(
            weight[mine, at],
            events[mine, at].astype(F32),
            local_one[mine, at] + widen(bases[mine, :], step),
            local_two[mine, at] + widen(bases[pl.ds(rows + group * GROUP, GROUP), :], step),
        )
        label = leaf[mine, at]
        low = (label & (LOW - 1)).astype(F32).astype(BF16)
        high = lax.shift_right_logical(label, LOW.bit_length() - 1).astype(F32).astype(BF16)
        terms = []
        for value in pair:
            upper = value.astype(BF16)
            terms += [upper, (value - upper.astype(F32)).astype(BF16)]
        if out is not None:
            out[0, mine, at_out] = terms[0]
            out[1, mine, at_out] = terms[2]
        left = jnp.concatenate([jnp.where(high == h, term, zero) for term in terms for h in range(HIGH)], axis=0)
        right = jnp.concatenate([jnp.where(low == k, unit, zero) for k in range(LOW)], axis=0)
        acc[group] += lax.dot_general(left, right, (((1,), (1,)), ((), ())), preferred_element_type=F32)


def leaf_shares(shares, size, meta, ins, outs, acc):
    step = min(size, 2048)
    for k, d in enumerate(shares):
        start = share_of(meta, d, size)

        def one(turn, carry):
            at = turn * step
            leaf_step(span(start + at, step), *ins, acc, outs[k] if k < len(outs) else None, span(at, step))
            return carry

        lax.fori_loop(0, size // step, one, 0, unroll=4)


def leaf_first_body(shares, size, meta, *refs):
    acc = refs[-1]
    acc[...] = jnp.zeros_like(acc)
    leaf_shares(shares, size, meta, refs[:6], refs[6:-1], acc)


def leaf_rest_body(shares, size, meta, *refs):
    own, sums, acc = refs[-3:]
    leaf_shares(shares, size, meta, refs[:6], [own], acc)
    width = LOW * GROUP
    side = HIGH * GROUP
    same = lax.broadcasted_iota(jnp.int32, (side, width), 0) % GROUP == lax.broadcasted_iota(jnp.int32, (side, width), 1) % GROUP
    source = lax.broadcasted_iota(jnp.int32, (width, LANES), 0) // GROUP
    target = lax.broadcasted_iota(jnp.int32, (width, LANES), 1)
    for group in range(acc.shape[0]):
        out = jnp.zeros((GROUP, LANES), F32)
        for value in (0, 1):
            both = acc[group, 2 * value * side : (2 * value + 1) * side] + acc[group, (2 * value + 1) * side : (2 * value + 2) * side]
            both = jnp.where(same, both, 0.0)
            for h in range(HIGH):
                place = (target == source + (h * LOW + value * LEAVES)).astype(F32)
                out = out + jnp.dot(
                    both[h * GROUP : (h + 1) * GROUP], place, precision=lax.Precision.HIGHEST, preferred_element_type=F32
                )
        sums[group * GROUP : (group + 1) * GROUP, :] = out


def update_body(turns, partners, meta, pred, leaf, *refs):
    arrived, refs = refs[: len(partners)], refs[len(partners) + 1 :]
    sums, (new_pred, leaf_weights, out, scratch, sems, piece_sems) = refs[:-6], refs[-6:]
    rows, length = leaf.shape
    copies = place_pieces(meta, partners, arrived, out, piece_sems)
    for copy in copies:
        copy.start()
    both = [ref[...] for ref in sums]
    while len(both) > 1:
        both = [a + b for a, b in zip(both[::2], both[1::2])]
    table = -both[0] / (pltpu.roll(both[0], LANES - LEAVES, 1) + 1.0)
    leaf_weights[...] = table[:, :LEAVES]
    width = length // turns
    step = min(width, 512)
    for turn in range(turns):

        def one(k, carry):
            at = span(turn * width + k * step, step)
            label = leaf[:, at]
            picked = [take(table, label[:, j : j + LANES]) for j in range(0, step, LANES)]
            scratch[:, at] = pred[:, at] + jnp.concatenate(picked, axis=1)
            return carry

        lax.fori_loop(0, width // step, one, 0, unroll=8)
        at = pl.ds(turn * width, width)
        copies.append(pltpu.make_async_copy(scratch.at[:, at], new_pred.at[:, at], sems.at[turn]))
        copies[-1].start()
    for copy in copies:
        copy.wait()


def swap(array, axis, d):
    return lax.ppermute(array, axis, [(i, i ^ d) for i in range(lax.axis_size(axis))])


def across(total, axis, arrived=()):
    mate = swap(total, axis, 1)
    (both,) = call(pair_body, [resident(total.shape, F32)], total, mate, *arrived, name="pair", us=0.3, limit=4)
    return both, [mate] + [swap(both, axis, d) for d in range(2, lax.axis_size(axis), 2)]


def on_device(predictions, leaf_index, events, tie_start):
    rows, length = predictions.shape
    blocks = length // LANES
    parts = lax.axis_size("ep")
    share = length // parts
    wide = (rows, length)
    turns = 8
    dma = pltpu.SemaphoreType.DMA
    tie = near(tie_start.reshape(blocks, LANES))
    meta = jnp.stack([lax.axis_index("ep"), lax.axis_index("tm")]).astype(jnp.int32)

    links = [d for d in range(1, parts) if d & (d - 1) == 0]
    diagonals = [d for d in range(1, parts) if d not in links]
    message = resident((2, rows, share), I16)
    observed, weight, total, *messages = call(
        functools.partial(front_body, links, turns, parts),
        [resident(wide, jnp.int32), resident(wide, F32), resident((rows, LANES), F32)] + [message] * len(links),
        meta,
        far(predictions),
        far(events),
        hbm=(1, 2),
        scratch=[pltpu.VMEM(wide, F32), dma((turns,)), dma((parts,))],
        name="front",
        us=4,
    )
    coded = {d: swap(m, "ep", d) for d, m in zip(links, messages)}
    _, from_later = across(total, "tm")
    suffix, grouped, last, leaf = call(
        scan_body,
        [
            resident(wide, F32),
            resident((rows // FIELDS, length), jnp.int32),
            resident((blocks, LANES), jnp.int32),
            resident(wide, jnp.int32),
        ],
        weight,
        observed,
        tie,
        far(leaf_index),
        hbm=(3,),
        scratch=[pltpu.VMEM((WIDE, WIDE), BF16)] * 2 + [dma],
        name="scan",
        us=5,
    )
    count = len(from_later)
    inv_one, inv_two, totals, after = call(
        functools.partial(inverse_body, count, parts),
        [resident(wide, F32), resident(wide, F32), resident((2 * rows, LANES), F32), resident((parts, rows, LANES), F32)],
        meta,
        *from_later,
        suffix,
        grouped,
        aliases={1 + count: 0},
        name="inverse",
        us=1.5,
    )
    _, from_earlier = across(totals, "tm")
    local_one, local_two, before = call(
        functools.partial(accum_body, parts),
        [resident(wide, F32), resident(wide, F32), resident((parts, 2 * rows, LANES), F32)],
        inv_one,
        inv_two,
        aliases={0: 0, 1: 1},
        scratch=[pltpu.VMEM((WIDE, WIDE), BF16)],
        name="accum",
        us=3,
    )
    scans = (weight, observed, local_one, local_two)
    bases, *sent = call(
        functools.partial(bases_body, count, links),
        [resident((2 * rows, LANES), F32)] + [resident((3 * rows, LANES), F32)] * len(links),
        meta,
        *from_earlier,
        after,
        before,
        name="bases",
        us=1,
    )
    base = {d: swap(m, "ep", d) for d, m in zip(links, sent)}
    finished = resident((2, rows, share), BF16)
    sums_shape = resident((rows // GROUP, 4 * HIGH * GROUP, LOW * GROUP), F32)
    *sent, acc = call(
        functools.partial(leaf_first_body, diagonals, share),
        [finished] * len(diagonals) + [sums_shape],
        meta,
        leaf,
        *scans,
        bases,
        name="leaf_first",
        us=3,
    )
    sent = call(
        release_body,
        [finished] * len(diagonals),
        *sent,
        *base.values(),
        *coded.values(),
        aliases={k: k for k in range(len(diagonals))},
        name="release",
        us=0.1,
        limit=2,
    )
    arrived = [swap(m, "ep", d) for d, m in zip(diagonals, sent)]
    own, own_sums, _ = call(
        functools.partial(leaf_rest_body, [0] + links, share),
        [finished, resident((rows, LANES), F32), sums_shape],
        meta,
        leaf,
        *scans,
        bases,
        acc,
        *sent,
        aliases={7: 2},
        name="leaf_rest",
        us=9,
    )
    both, others = across(own_sums, "tm", base.values())
    piece = pltpu.VMEM((len(links), rows, share), F32)
    args = [meta, tie, last, *[coded[d] for d in links], *[base[d] for d in links], own]
    grad_hess, pred = call(
        functools.partial(finish_body, links),
        [jax.ShapeDtypeStruct((2, rows * parts, share), BF16), resident(wide, F32)],
        *args,
        far(predictions),
        hbm=(len(args),),
        hbm_out=(0,),
        scratch=[pltpu.VMEM((len(links), 2, rows, share), BF16)]
        + [piece] * 3
        + [pltpu.VMEM((WIDE, WIDE), BF16)] * 2
        + [dma((len(links), 2, 4)), dma((1, 2)), dma],
        name="finish",
        us=8,
        limit=14,
    )
    at_out = 3 + len(diagonals)
    new_pred, leaf_weights, grad_hess = call(
        functools.partial(update_body, turns, diagonals),
        [jax.ShapeDtypeStruct(wide, F32), jax.ShapeDtypeStruct((rows, LEAVES), F32), jax.ShapeDtypeStruct(grad_hess.shape, BF16)],
        meta,
        pred,
        leaf,
        *arrived,
        grad_hess,
        both,
        *others[1:],
        hbm=range(3, at_out + 1),
        hbm_out=(0, 2),
        aliases={at_out: 2},
        scratch=[pltpu.VMEM(wide, F32), dma((turns,)), dma((max(1, len(diagonals)), 2))],
        name="update",
        us=4,
    )
    return new_pred, leaf_weights, grad_hess.reshape(2, rows * parts, 1, share)


def solution(mesh):
    placed = (P("ep", "tm"), P("ep", "tm"), P("ep", "tm"), P("tm"))
    return jax.shard_map(
        on_device,
        mesh=mesh,
        in_specs=placed,
        out_specs=(P("ep", "tm"), P("ep", None), P(None, None, "tm", "ep")),
        check_vma=False,
    )
```

```python
import functools
import math

import jax
import jax.numpy as jnp
from jax import lax
from jax.experimental import pallas as pl
from jax.experimental.pallas import tpu as pltpu
from jax.sharding import PartitionSpec as P

LEAVES = 64
LANES = 128
WIDE = 256
F32 = jnp.float32
BF16 = jnp.bfloat16
I16 = jnp.int16
CODE = 32766.0 / 6.0
MIDDLE = 32768
MIB = 1024 * 1024
PIECE = 2048


def resident(shape, dtype):
    return pltpu.VMEM(shape, dtype)


def near(array):
    return pltpu.with_memory_space_constraint(array, pltpu.VMEM)


def far(array):
    return pltpu.with_memory_space_constraint(array, pltpu.HBM)


def call(body, outs, *args, scratch=(), name=None, us=1.0, aliases=None, limit=12, hbm=(), hbm_out=()):
    vmem = pl.BlockSpec(memory_space=pltpu.VMEM)
    smem = pl.BlockSpec(memory_space=pltpu.SMEM)
    anywhere = pl.BlockSpec(memory_space=pltpu.HBM)
    return pl.pallas_call(
        body,
        out_shape=outs,
        in_specs=[anywhere if k in hbm else smem if a.ndim == 1 else vmem for k, a in enumerate(args)],
        out_specs=[anywhere if k in hbm_out else vmem for k in range(len(outs))],
        scratch_shapes=list(scratch),
        input_output_aliases=aliases or {},
        compiler_params=pltpu.CompilerParams(vmem_limit_bytes=limit * MIB),
        cost_estimate=pl.CostEstimate(flops=0, bytes_accessed=int(us * 3.5e6), transcendentals=0),
        name=name,
    )(*args)


def lane_sum(x):
    return jnp.broadcast_to(jnp.sum(x, axis=1, keepdims=True), (x.shape[0], LANES))


def fold(x):
    parts = [x[:, k : k + LANES] for k in range(0, x.shape[1], LANES)]
    while len(parts) > 1:
        parts = [a + b for a, b in zip(parts[::2], parts[1::2])] + parts[len(parts) & ~1 :]
    return parts[0]


def span(start, size):
    return pl.ds(pl.multiple_of(start, size), size)


def widen(x, step):
    return jnp.concatenate([x] * (step // LANES), axis=1)


def share_of(meta, d, size):
    return (meta[0] ^ d) * size


def encode(meta, d, pred, events, message):
    share = message.shape[2]
    step = min(share, 1024)

    def one(turn, carry):
        source = span(share_of(meta, d, share) + turn * step, step)
        at = span(turn * step, step)
        above = (pred[:, source] * CODE + (MIDDLE + 0.5)).astype(jnp.int32)
        message[0, :, at] = (above - MIDDLE).astype(I16)
        message[1, :, at] = events[:, source].astype(I16)
        return carry

    lax.fori_loop(0, share // step, one, 0, unroll=2)


def front_body(partners, turns, parts, meta, pred_in, events_in, events, weight, total, *rest):
    messages, pred, sems, share_sems = rest[:-3], rest[-3], rest[-2], rest[-1]
    rows, length = pred.shape
    width = length // turns
    share = length // parts
    loads = []
    for turn in range(turns):
        at = span(turn * width, width)
        loads.append(pltpu.make_async_copy(pred_in.at[:, at], pred.at[:, at], sems.at[turn]))
    order = list(partners) + [d for d in range(parts) if d not in partners]
    fetches = []
    for k, d in enumerate(order):
        at = span(share_of(meta, d, share), share)
        fetches.append(pltpu.make_async_copy(events_in.at[:, at], events.at[:, at], share_sems.at[k]))
    for copy in loads + fetches:
        copy.start()
    step = min(width, 1024)
    acc = jnp.zeros((rows, LANES), F32)
    for turn in range(turns):
        loads[turn].wait()

        def one(k, acc):
            at = span(turn * width + k * step, step)
            value = jnp.exp(pred[:, at])
            weight[:, at] = value
            return acc + fold(value)

        acc = lax.fori_loop(0, width // step, one, acc, unroll=2)
    total[...] = lane_sum(acc)
    for k, (d, message) in enumerate(zip(partners, messages)):
        fetches[k].wait()
        encode(meta, d, pred, events, message)
    for copy in fetches[len(partners) :]:
        copy.wait()


def scan_matrix(backward):
    above = lax.broadcasted_iota(jnp.int32, (WIDE, WIDE), 0) % LANES
    along = lax.broadcasted_iota(jnp.int32, (WIDE, WIDE), 1)
    inside = above >= along if backward else above <= along
    return (inside | (along >= LANES)).astype(BF16)


def block_sums(x, matrix):
    high = x.astype(BF16)
    low = (x - high.astype(F32)).astype(BF16)
    both = jnp.dot(jnp.concatenate([high, low], axis=1), matrix, preferred_element_type=F32)
    return both[:, :LANES], both[:, LANES:]


def take(x, index):
    return jnp.take_along_axis(x, index, axis=1, mode="promise_in_bounds")


def last_in_group(starts):
    lane = lax.broadcasted_iota(jnp.int32, starts.shape, 1)
    after = pltpu.roll(starts, LANES - 1, 1)
    best = jnp.where((after == 1) | (lane == LANES - 1), lane, LANES - 1)
    for shift in (1, 2, 4, 8, 16, 32, 64):
        moved = pltpu.roll(best, LANES - shift, 1)
        best = jnp.where(lane < LANES - shift, jnp.minimum(best, moved), best)
    return best


def triangle(backward):
    above = lax.broadcasted_iota(jnp.int32, (WIDE, WIDE), 0)
    along = lax.broadcasted_iota(jnp.int32, (WIDE, WIDE), 1)
    return (above >= along if backward else above <= along).astype(BF16)


def stacked(ref, base, count, width=WIDE):
    return jnp.concatenate([ref[:, span(base + k * width, width)] for k in range(count)], axis=0)


FIELDS = 4
BITS = 8


def pack(x):
    size = x.shape[0] // FIELDS
    out = x[:size]
    for k in range(1, FIELDS):
        out = out + lax.shift_left(x[k * size : (k + 1) * size], BITS * k)
    return out


def unpack(x):
    return jnp.concatenate([(lax.shift_right_logical(x, BITS * k) & 255).astype(F32) for k in range(FIELDS)], axis=0)


def group_events(observed, counts, first, last):
    held = pack(counts.astype(jnp.int32))
    return jnp.where(first == 1, take(held, last) - held + pack(observed), 0)


def scan_body(weight, events, tie, leaf_in, suffix, grouped, last, leaf, upper, lower, sem):
    rows, length = weight.shape
    fetch = pltpu.make_async_copy(leaf_in, leaf, sem)
    fetch.start()
    count = min(16, length // WIDE)
    last[...] = last_in_group(tie[...])
    upper[...] = scan_matrix(True)
    lower[...] = triangle(False)
    steps = length // (WIDE * count)

    def one(turn, carry):
        base = (steps - 1 - turn) * (WIDE * count)
        observed = stacked(events, base, count)
        counts = jnp.dot(observed.astype(F32).astype(BF16), lower[...], preferred_element_type=F32)
        summed, totals = block_sums(stacked(weight, base, 2 * count, LANES), upper[...])
        for k in range(count - 1, -1, -1):
            mine = slice(k * rows, (k + 1) * rows)
            for half in (1, 0):
                lanes = slice(half * LANES, (half + 1) * LANES)
                at = span(base + k * WIDE + half * LANES, LANES)
                block = pl.ds((base + k * WIDE) // LANES + half, 1)
                here = slice((2 * k + half) * rows, (2 * k + half + 1) * rows)
                suffix[:, at] = summed[here] + carry
                carry = carry + totals[here]
                grouped[:, at] = group_events(
                    observed[mine, lanes],
                    counts[mine, lanes],
                    jnp.broadcast_to(tie[block, :], (rows // FIELDS, LANES)),
                    jnp.broadcast_to(last[block, :], (rows // FIELDS, LANES)),
                )
        return carry

    lax.fori_loop(0, steps, one, jnp.zeros((rows, LANES), F32), unroll=2)
    fetch.wait()


def pair_body(left, right, *refs):
    refs[-1][...] = left[...] + right[...]


def gathered_sum(meta, refs, later):
    mine = meta[1]
    out = None
    for k, ref in enumerate(refs):
        other = mine ^ (1 if k == 0 else 2 * k)
        wanted = (other > mine) if later else (other < mine)
        term = ref[...] * wanted.astype(F32)
        out = term if out is None else out + term
    return out


def inverse_body(count, parts, *refs):
    meta, others = refs[0], refs[1 : 1 + count]
    suffix, grouped, inv_one, inv_two, totals, after = refs[1 + count :]
    rows, length = suffix.shape
    share = length // parts
    later = gathered_sum(meta, others, True)
    for part in range(parts - 1):
        after[part] = jnp.broadcast_to(suffix[:, (part + 1) * share : (part + 1) * share + 1], (rows, LANES)) + later
    after[parts - 1] = later
    step = min(length, 512)

    def one(turn, acc):
        sum_one, sum_two = acc
        at = span(turn * step, step)
        inverse = 1.0 / (suffix[:, at] + widen(later, step))
        first = unpack(grouped[:, at]) * inverse
        second = first * inverse
        inv_one[:, at] = first
        inv_two[:, at] = second
        return (sum_one + fold(first), sum_two + fold(second))

    empty = jnp.zeros((rows, LANES), F32)
    sum_one, sum_two = lax.fori_loop(0, length // step, one, (empty, empty), unroll=2)
    totals[:rows, :] = lane_sum(sum_one)
    totals[rows:, :] = lane_sum(sum_two)


def accum_body(parts, inv_one, inv_two, one_out, two_out, before, lower):
    rows, length = inv_one.shape
    share = length // parts
    count = min(16, share // WIDE)
    lower[...] = scan_matrix(False)
    empty = jnp.zeros((rows, LANES), F32)
    carry = (empty, empty)
    for part in range(parts):
        before[part, :rows] = carry[0]
        before[part, rows:] = carry[1]

        def one(turn, carry):
            base = part * share + turn * (WIDE * count)
            made = []
            for ref, out, so_far in ((inv_one, one_out, carry[0]), (inv_two, two_out, carry[1])):
                summed, totals = block_sums(stacked(ref, base, 2 * count, LANES), lower[...])
                for k in range(2 * count):
                    mine = slice(k * rows, (k + 1) * rows)
                    out[:, span(base + k * LANES, LANES)] = summed[mine] + so_far
                    so_far = so_far + totals[mine]
                made.append(so_far)
            return tuple(made)

        carry = lax.fori_loop(0, share // (WIDE * count), one, carry, unroll=2)


def derivatives(weight, observed, accum_one, accum_two):
    scaled = weight * accum_one
    return scaled - observed, scaled - weight * weight * accum_two


def bases_body(count, links, *refs):
    meta, others = refs[0], refs[1 : 1 + count]
    after, before = refs[1 + count : 3 + count]
    bases, *messages = refs[len(refs) - 1 - len(links) :]
    rows = after.shape[1]
    earlier = gathered_sum(meta, others, False)
    bases[...] = earlier
    for d, message in zip(links, messages):
        part = share_of(meta, d, 1)
        message[:rows] = after[part]
        message[rows:] = before[part] + earlier


def release_body(*refs):
    pass


def place_pieces(meta, partners, arrived, out, sems):
    copies = []
    for k, (d, piece) in enumerate(zip(partners, arrived)):
        rows = piece.shape[1]
        where = pl.ds(pl.multiple_of(share_of(meta, d, rows), rows), rows)
        copies += [pltpu.make_async_copy(piece.at[v], out.at[v, where, :], sems.at[k, v]) for v in (0, 1)]
    return copies


def partner_scan(turn, slot, message, so_far, first_block, tie, last, upper, lower, kept, inv_one, inv_two):
    _, rows, share = kept.shape
    steps = share // PIECE
    count = PIECE // WIDE
    at_base = (steps - 1 - turn) * PIECE
    coded = jnp.concatenate([message[0, :, span(at_base + k * WIDE, WIDE)] for k in range(count)], axis=0)
    values = jnp.exp(coded.astype(jnp.int32).astype(F32) * (1.0 / CODE))
    seen = jnp.concatenate([message[1, :, span(at_base + k * WIDE, WIDE)] for k in range(count)], axis=0)
    observed = seen.astype(jnp.int32)
    counts = jnp.dot(observed.astype(F32).astype(BF16), lower[...], preferred_element_type=F32)
    blocks = [values[k * rows : (k + 1) * rows, half * LANES : (half + 1) * LANES] for k in range(count) for half in (0, 1)]
    summed, totals = block_sums(jnp.concatenate(blocks, axis=0), upper[...])
    for k in range(count - 1, -1, -1):
        mine = slice(k * rows, (k + 1) * rows)
        kept[slot, :, span(at_base + k * WIDE, WIDE)] = values[mine]
        for half in (1, 0):
            here = slice((2 * k + half) * rows, (2 * k + half + 1) * rows)
            lanes = slice(half * LANES, (half + 1) * LANES)
            at = span(at_base + k * WIDE + half * LANES, LANES)
            block = pl.ds(first_block + (at_base + k * WIDE) // LANES + half, 1)
            grouped = group_events(
                observed[mine, lanes],
                counts[mine, lanes],
                jnp.broadcast_to(tie[block, :], (rows // FIELDS, LANES)),
                jnp.broadcast_to(last[block, :], (rows // FIELDS, LANES)),
            )
            inverse = 1.0 / (summed[here] + so_far)
            so_far = so_far + totals[here]
            first = unpack(grouped) * inverse
            inv_one[slot, :, at] = first
            inv_two[slot, :, at] = first * inverse
    return so_far


def finish_body(partners, *refs):
    meta, refs = refs[0], refs[1:]
    messages, base = refs[: len(partners)], refs[len(partners) : 2 * len(partners)]
    own, kept, inv_one, inv_two, pred_in, out, pred, scratch, lower, sems, own_sems, fetch_sem = refs[2 * len(partners) :]
    fetch = pltpu.make_async_copy(pred_in, pred, fetch_sem)
    fetch.start()
    own_copies = place_pieces(meta, [0], [own], out, own_sems)
    for copy in own_copies:
        copy.start()
    _, rows, share = kept.shape
    steps = share // PIECE
    count = PIECE // WIDE
    lower[...] = scan_matrix(False)

    def copies(turn):
        lanes = span(turn * PIECE, PIECE)
        made = []
        for slot, d in enumerate(partners):
            where = pl.ds(pl.multiple_of(share_of(meta, d, rows), rows), rows)
            made += [
                pltpu.make_async_copy(scratch.at[slot, v, :, lanes], out.at[v, where, lanes], sems.at[slot, v, turn])
                for v in (0, 1)
            ]
        return made

    def one(turn, carry):
        at_base = turn * PIECE
        made = []
        for slot in range(len(partners)):
            sum_one, total_one = block_sums(stacked(inv_one.at[slot], at_base, 2 * count, LANES), lower[...])
            sum_two, total_two = block_sums(stacked(inv_two.at[slot], at_base, 2 * count, LANES), lower[...])
            so_one, so_two = carry[slot]
            for k in range(2 * count):
                mine = slice(k * rows, (k + 1) * rows)
                at = span(at_base + k * LANES, LANES)
                grad, hess = derivatives(
                    kept[slot, :, at],
                    messages[slot][1, :, at].astype(jnp.int32).astype(F32),
                    sum_one[mine] + so_one,
                    sum_two[mine] + so_two,
                )
                scratch[slot, 0, :, at] = grad.astype(BF16)
                scratch[slot, 1, :, at] = hess.astype(BF16)
                so_one = so_one + total_one[mine]
                so_two = so_two + total_two[mine]
            made.append((so_one, so_two))
        for copy in copies(turn):
            copy.start()
        return tuple(made)

    lax.fori_loop(0, steps, one, tuple((b[rows : 2 * rows, :], b[2 * rows :, :]) for b in base))
    for turn in range(steps):
        for copy in copies(turn):
            copy.wait()
    for copy in own_copies:
        copy.wait()
    fetch.wait()


GROUP = 16
LOW = 16
HIGH = LEAVES // LOW


def leaf_step(at, leaf, weight, events, local_one, local_two, bases, acc, out, at_out):
    rows = weight.shape[0]
    step = at.size
    zero = jnp.zeros((GROUP, step), BF16)
    unit = jnp.ones((GROUP, step), BF16)
    for group in range(rows // GROUP):
        mine = pl.ds(group * GROUP, GROUP)
        pair = derivatives(
            weight[mine, at],
            events[mine, at].astype(F32),
            local_one[mine, at] + widen(bases[mine, :], step),
            local_two[mine, at] + widen(bases[pl.ds(rows + group * GROUP, GROUP), :], step),
        )
        label = leaf[mine, at]
        low = (label & (LOW - 1)).astype(F32).astype(BF16)
        high = lax.shift_right_logical(label, LOW.bit_length() - 1).astype(F32).astype(BF16)
        terms = []
        for value in pair:
            upper = value.astype(BF16)
            terms += [upper, (value - upper.astype(F32)).astype(BF16)]
        if out is not None:
            out[0, mine, at_out] = terms[0]
            out[1, mine, at_out] = terms[2]
        left = jnp.concatenate([jnp.where(high == h, term, zero) for term in terms for h in range(HIGH)], axis=0)
        right = jnp.concatenate([jnp.where(low == k, unit, zero) for k in range(LOW)], axis=0)
        acc[group] += lax.dot_general(left, right, (((1,), (1,)), ((), ())), preferred_element_type=F32)


def leaf_first_body(shares, size, meta, *refs):
    ins, outs, acc = refs[:6], refs[6:-1], refs[-1]
    acc[...] = jnp.zeros_like(acc)
    for d, out in zip(shares, outs):
        start = share_of(meta, d, size)

        def one(turn, carry):
            leaf_step(span(start + turn * PIECE, PIECE), *ins, acc, out, span(turn * PIECE, PIECE))
            return carry

        lax.fori_loop(0, size // PIECE, one, 0, unroll=4)


def leaf_rest_body(links, size, meta, *refs):
    ins, tie, last = refs[:6], refs[6], refs[7]
    messages, base = refs[8 : 8 + len(links)], refs[8 + len(links) : 8 + 2 * len(links)]
    own, sums, kept, inv_one, inv_two, acc, upper, lower = refs[-8:]
    upper[...] = scan_matrix(True)
    lower[...] = triangle(False)
    rows = kept.shape[1]
    first_block = share_of(meta, 0, size) // LANES

    def one(turn, carry):
        at = turn * PIECE
        made = []
        leaf_step(span(share_of(meta, 0, size) + at, PIECE), *ins, acc, own, span(at, PIECE))
        for slot, d in enumerate(links):
            made.append(
                partner_scan(
                    turn, slot, messages[slot], carry[slot], first_block, tie, last, upper, lower, kept, inv_one, inv_two
                )
            )
            leaf_step(span(share_of(meta, d, size) + at, PIECE), *ins, acc, None, None)
        return tuple(made)

    lax.fori_loop(0, size // PIECE, one, tuple(b[:rows, :] for b in base))
    width = LOW * GROUP
    side = HIGH * GROUP
    same = lax.broadcasted_iota(jnp.int32, (side, width), 0) % GROUP == lax.broadcasted_iota(jnp.int32, (side, width), 1) % GROUP
    held = []
    for group in range(rows // GROUP):
        for value in (0, 1):
            both = acc[group, 2 * value * side : (2 * value + 1) * side] + acc[group, (2 * value + 1) * side : (2 * value + 2) * side]
            held.append(jnp.where(same, both, 0.0))
    held = jnp.concatenate(held, axis=0)
    source = lax.broadcasted_iota(jnp.int32, (width, LANES), 0) // GROUP
    place = (source == lax.broadcasted_iota(jnp.int32, (width, LANES), 1)).astype(BF16)
    by_low = jnp.zeros((held.shape[0], LANES), F32)
    for _ in range(3):
        part = held.astype(BF16)
        held = held - part.astype(F32)
        by_low = by_low + jnp.dot(part, place, preferred_element_type=F32)
    for group in range(rows // GROUP):
        out = jnp.zeros((GROUP, LANES), F32)
        for value in (0, 1):
            for h in range(HIGH):
                at = ((group * 2 + value) * HIGH + h) * GROUP
                out = out + pltpu.roll(by_low[at : at + GROUP], h * LOW + value * LEAVES, 1)
        sums[group * GROUP : (group + 1) * GROUP, :] = out


def place_body(partners, cuts, meta, *refs):
    out, sems = refs[-2:]
    copies = []
    for k, (d, piece) in enumerate(zip(partners, refs)):
        _, rows, size = piece.shape
        where = pl.ds(pl.multiple_of(share_of(meta, d, rows), rows), rows)
        for v in (0, 1):
            for cut in range(cuts):
                lanes = pl.ds(cut * (size // cuts), size // cuts)
                copies.append(pltpu.make_async_copy(piece.at[v, :, lanes], out.at[v, where, lanes], sems.at[k, v, cut]))
    for copy in copies:
        copy.start()
    for copy in copies:
        copy.wait()


def update_body(turns, pred, leaf, *refs):
    sums, (new_pred, leaf_weights, scratch, weights, sems) = refs[:-5], refs[-5:]
    rows, length = leaf.shape
    both = [ref[...] for ref in sums]
    while len(both) > 1:
        both = [a + b for a, b in zip(both[::2], both[1::2])]
    table = -both[0] / (pltpu.roll(both[0], LANES - LEAVES, 1) + 1.0)
    weights[...] = table[:, :LEAVES]
    copies = [pltpu.make_async_copy(weights, leaf_weights, sems.at[turns])]
    copies[0].start()
    width = length // turns
    step = min(width, 512)
    for turn in range(turns):

        def one(k, carry):
            at = span(turn * width + k * step, step)
            label = leaf[:, at]
            picked = [take(table, label[:, j : j + LANES]) for j in range(0, step, LANES)]
            scratch[:, at] = pred[:, at] + jnp.concatenate(picked, axis=1)
            return carry

        lax.fori_loop(0, width // step, one, 0, unroll=8)
        at = pl.ds(turn * width, width)
        copies.append(pltpu.make_async_copy(scratch.at[:, at], new_pred.at[:, at], sems.at[turn]))
        copies[-1].start()
    for copy in copies:
        copy.wait()


def swap(array, axis, d):
    return lax.ppermute(array, axis, [(i, i ^ d) for i in range(lax.axis_size(axis))])


def across(total, axis, arrived=()):
    mate = swap(total, axis, 1)
    (both,) = call(pair_body, [resident(total.shape, F32)], total, mate, *arrived, name="pair", us=0.3, limit=4)
    return both, [mate] + [swap(both, axis, d) for d in range(2, lax.axis_size(axis), 2)]


def on_device(predictions, leaf_index, events, tie_start):
    rows, length = predictions.shape
    blocks = length // LANES
    parts = lax.axis_size("ep")
    share = length // parts
    wide = (rows, length)
    turns = 8
    dma = pltpu.SemaphoreType.DMA
    tie = near(tie_start.reshape(blocks, LANES))
    meta = jnp.stack([lax.axis_index("ep"), lax.axis_index("tm")]).astype(jnp.int32)

    links = [d for d in range(1, parts) if d & (d - 1) == 0]
    diagonals = [d for d in range(1, parts) if d not in links]
    message = resident((2, rows, share), I16)
    observed, weight, total, *messages = call(
        functools.partial(front_body, links, turns, parts),
        [resident(wide, jnp.int32), resident(wide, F32), resident((rows, LANES), F32)] + [message] * len(links),
        meta,
        far(predictions),
        far(events),
        hbm=(1, 2),
        scratch=[pltpu.VMEM(wide, F32), dma((turns,)), dma((parts,))],
        name="front",
        us=4,
    )
    coded = {d: swap(m, "ep", d) for d, m in zip(links, messages)}
    _, from_later = across(total, "tm")
    suffix, grouped, last, leaf = call(
        scan_body,
        [
            resident(wide, F32),
            resident((rows // FIELDS, length), jnp.int32),
            resident((blocks, LANES), jnp.int32),
            resident(wide, jnp.int32),
        ],
        weight,
        observed,
        tie,
        far(leaf_index),
        hbm=(3,),
        scratch=[pltpu.VMEM((WIDE, WIDE), BF16)] * 2 + [dma],
        name="scan",
        us=5,
    )
    count = len(from_later)
    inv_one, inv_two, totals, after = call(
        functools.partial(inverse_body, count, parts),
        [resident(wide, F32), resident(wide, F32), resident((2 * rows, LANES), F32), resident((parts, rows, LANES), F32)],
        meta,
        *from_later,
        suffix,
        grouped,
        aliases={1 + count: 0},
        name="inverse",
        us=1.5,
    )
    _, from_earlier = across(totals, "tm")
    local_one, local_two, before = call(
        functools.partial(accum_body, parts),
        [resident(wide, F32), resident(wide, F32), resident((parts, 2 * rows, LANES), F32)],
        inv_one,
        inv_two,
        aliases={0: 0, 1: 1},
        scratch=[pltpu.VMEM((WIDE, WIDE), BF16)],
        name="accum",
        us=3,
    )
    scans = (weight, observed, local_one, local_two)
    bases, *sent = call(
        functools.partial(bases_body, count, links),
        [resident((2 * rows, LANES), F32)] + [resident((3 * rows, LANES), F32)] * len(links),
        meta,
        *from_earlier,
        after,
        before,
        name="bases",
        us=1,
    )
    base = {d: swap(m, "ep", d) for d, m in zip(links, sent)}
    finished = resident((2, rows, share), BF16)
    sums_shape = resident((rows // GROUP, 4 * HIGH * GROUP, LOW * GROUP), F32)
    *sent, acc = call(
        functools.partial(leaf_first_body, diagonals, share),
        [finished] * len(diagonals) + [sums_shape],
        meta,
        leaf,
        *scans,
        bases,
        name="leaf_first",
        us=3,
    )
    sent = call(
        release_body,
        [finished] * len(diagonals),
        *sent,
        *base.values(),
        *coded.values(),
        aliases={k: k for k in range(len(diagonals))},
        name="release",
        us=0.1,
        limit=2,
    )
    arrived = [swap(m, "ep", d) for d, m in zip(diagonals, sent)]
    piece = resident((len(links), rows, share), F32)
    received = [*[coded[d] for d in links], *[base[d] for d in links]]
    args = [meta, leaf, *scans, bases, tie, last, *received]
    own, own_sums, *held, _ = call(
        functools.partial(leaf_rest_body, links, share),
        [finished, resident((rows, LANES), F32)] + [piece] * 3 + [sums_shape],
        *args,
        acc,
        *sent,
        aliases={len(args): 5},
        scratch=[pltpu.VMEM((WIDE, WIDE), BF16)] * 2,
        name="leaf_rest",
        us=10,
        limit=16,
    )
    both, others = across(own_sums, "tm", base.values())
    args = [meta, *received, own, *held]
    grad_hess, pred = call(
        functools.partial(finish_body, links),
        [jax.ShapeDtypeStruct((2, rows * parts, share), BF16), resident(wide, F32)],
        *args,
        far(predictions),
        hbm=(len(args),),
        hbm_out=(0,),
        scratch=[
            pltpu.VMEM((len(links), 2, rows, share), BF16),
            pltpu.VMEM((WIDE, WIDE), BF16),
            dma((len(links), 2, share // PIECE)),
            dma((1, 2)),
            dma,
        ],
        name="finish",
        us=4,
        limit=10,
    )
    new_pred, leaf_weights = call(
        functools.partial(update_body, turns),
        [jax.ShapeDtypeStruct(wide, F32), jax.ShapeDtypeStruct((rows, LEAVES), F32)],
        pred,
        leaf,
        both,
        *others[1:],
        hbm_out=(0, 1),
        scratch=[pltpu.VMEM(wide, F32), pltpu.VMEM((rows, LEAVES), F32), dma((turns + 1,))],
        name="update",
        us=4,
    )
    cuts = 4
    (grad_hess,) = call(
        functools.partial(place_body, diagonals, cuts),
        [jax.ShapeDtypeStruct(grad_hess.shape, BF16)],
        meta,
        *[near(x) for x in arrived],
        grad_hess,
        far(new_pred),
        hbm=(1 + len(arrived), 2 + len(arrived)),
        hbm_out=(0,),
        aliases={1 + len(arrived): 0},
        scratch=[dma((max(1, len(arrived)), 2, cuts))],
        name="place",
        us=1,
        limit=2,
    )
    return new_pred, leaf_weights, grad_hess.reshape(2, rows * parts, 1, share)


def solution(mesh):
    placed = (P("ep", "tm"), P("ep", "tm"), P("ep", "tm"), P("tm"))
    return jax.shard_map(
        on_device,
        mesh=mesh,
        in_specs=placed,
        out_specs=(P("ep", "tm"), P("ep", None), P(None, None, "tm", "ep")),
        check_vma=False,
    )
```

```python
import functools
import math

import jax
import jax.numpy as jnp
from jax import lax
from jax.experimental import pallas as pl
from jax.experimental.pallas import tpu as pltpu
from jax.sharding import PartitionSpec as P

LEAVES = 64
LANES = 128
WIDE = 256
F32 = jnp.float32
BF16 = jnp.bfloat16
I16 = jnp.int16
CODE = 32766.0 / 6.0
MIDDLE = 32768
MIB = 1024 * 1024
PIECE = 2048


def resident(shape, dtype):
    return pltpu.VMEM(shape, dtype)


def near(array):
    return pltpu.with_memory_space_constraint(array, pltpu.VMEM)


def far(array):
    return pltpu.with_memory_space_constraint(array, pltpu.HBM)


def call(body, outs, *args, scratch=(), name=None, us=1.0, aliases=None, limit=8, hbm=(), hbm_out=()):
    vmem = pl.BlockSpec(memory_space=pltpu.VMEM)
    smem = pl.BlockSpec(memory_space=pltpu.SMEM)
    anywhere = pl.BlockSpec(memory_space=pltpu.HBM)
    return pl.pallas_call(
        body,
        out_shape=outs,
        in_specs=[anywhere if k in hbm else smem if a.ndim == 1 else vmem for k, a in enumerate(args)],
        out_specs=[anywhere if k in hbm_out else vmem for k in range(len(outs))],
        scratch_shapes=list(scratch),
        input_output_aliases=aliases or {},
        compiler_params=pltpu.CompilerParams(vmem_limit_bytes=limit * MIB),
        cost_estimate=pl.CostEstimate(flops=0, bytes_accessed=int(us * 3.5e6), transcendentals=0),
        name=name,
    )(*args)


def lane_sum(x):
    return jnp.broadcast_to(jnp.sum(x, axis=1, keepdims=True), (x.shape[0], LANES))


def fold(x):
    parts = [x[:, k : k + LANES] for k in range(0, x.shape[1], LANES)]
    while len(parts) > 1:
        parts = [a + b for a, b in zip(parts[::2], parts[1::2])] + parts[len(parts) & ~1 :]
    return parts[0]


def span(start, size):
    return pl.ds(pl.multiple_of(start, size), size)


def widen(x, step):
    return jnp.concatenate([x] * (step // LANES), axis=1)


def share_of(meta, d, size):
    return (meta[0] ^ d) * size


def encode(meta, d, pred, events, message):
    share = message.shape[2]
    step = min(share, 1024)

    def one(turn, carry):
        source = span(share_of(meta, d, share) + turn * step, step)
        at = span(turn * step, step)
        above = (pred[:, source] * CODE + (MIDDLE + 0.5)).astype(jnp.int32)
        message[0, :, at] = (above - MIDDLE).astype(I16)
        message[1, :, at] = events[:, source].astype(I16)
        return carry

    lax.fori_loop(0, share // step, one, 0, unroll=2)


def front_body(partners, turns, parts, meta, pred_in, events_in, events, weight, total, *rest):
    messages, pred, sems, share_sems = rest[:-3], rest[-3], rest[-2], rest[-1]
    rows, length = pred.shape
    width = length // turns
    share = length // parts
    loads = []
    for turn in range(turns):
        at = span(turn * width, width)
        loads.append(pltpu.make_async_copy(pred_in.at[:, at], pred.at[:, at], sems.at[turn]))
    order = list(partners) + [d for d in range(parts) if d not in partners]
    fetches = []
    for k, d in enumerate(order):
        at = span(share_of(meta, d, share), share)
        fetches.append(pltpu.make_async_copy(events_in.at[:, at], events.at[:, at], share_sems.at[k]))
    for copy in loads + fetches:
        copy.start()
    step = min(width, 1024)
    acc = jnp.zeros((rows, LANES), F32)
    for turn in range(turns):
        loads[turn].wait()

        def one(k, acc):
            at = span(turn * width + k * step, step)
            value = jnp.exp(pred[:, at])
            weight[:, at] = value
            return acc + fold(value)

        acc = lax.fori_loop(0, width // step, one, acc, unroll=2)
    total[...] = lane_sum(acc)
    for k, (d, message) in enumerate(zip(partners, messages)):
        fetches[k].wait()
        encode(meta, d, pred, events, message)
    for copy in fetches[len(partners) :]:
        copy.wait()


def scan_matrix(backward):
    above = lax.broadcasted_iota(jnp.int32, (WIDE, WIDE), 0) % LANES
    along = lax.broadcasted_iota(jnp.int32, (WIDE, WIDE), 1)
    inside = above >= along if backward else above <= along
    return (inside | (along >= LANES)).astype(BF16)


def block_sums(x, matrix):
    high = x.astype(BF16)
    low = (x - high.astype(F32)).astype(BF16)
    both = jnp.dot(jnp.concatenate([high, low], axis=1), matrix, preferred_element_type=F32)
    return both[:, :LANES], both[:, LANES:]


def take(x, index):
    return jnp.take_along_axis(x, index, axis=1, mode="promise_in_bounds")


def last_in_group(starts):
    lane = lax.broadcasted_iota(jnp.int32, starts.shape, 1)
    after = pltpu.roll(starts, LANES - 1, 1)
    best = jnp.where((after == 1) | (lane == LANES - 1), lane, LANES - 1)
    for shift in (1, 2, 4, 8, 16, 32, 64):
        moved = pltpu.roll(best, LANES - shift, 1)
        best = jnp.where(lane < LANES - shift, jnp.minimum(best, moved), best)
    return best


def triangle(backward):
    above = lax.broadcasted_iota(jnp.int32, (WIDE, WIDE), 0)
    along = lax.broadcasted_iota(jnp.int32, (WIDE, WIDE), 1)
    return (above >= along if backward else above <= along).astype(BF16)


def stacked(ref, base, count, width=WIDE):
    return jnp.concatenate([ref[:, span(base + k * width, width)] for k in range(count)], axis=0)


FIELDS = 4
BITS = 8


def pack(x):
    size = x.shape[0] // FIELDS
    out = x[:size]
    for k in range(1, FIELDS):
        out = out + lax.shift_left(x[k * size : (k + 1) * size], BITS * k)
    return out


def unpack(x):
    return jnp.concatenate([(lax.shift_right_logical(x, BITS * k) & 255).astype(F32) for k in range(FIELDS)], axis=0)


def group_events(observed, counts, first, last):
    held = pack(counts.astype(jnp.int32))
    return jnp.where(first == 1, take(held, last) - held + pack(observed), 0)


def scan_body(weight, events, tie, leaf_in, suffix, grouped, last, leaf, upper, lower, sem):
    rows, length = weight.shape
    fetch = pltpu.make_async_copy(leaf_in, leaf, sem)
    fetch.start()
    count = min(16, length // WIDE)
    last[...] = last_in_group(tie[...])
    upper[...] = scan_matrix(True)
    lower[...] = triangle(False)
    steps = length // (WIDE * count)

    def one(turn, carry):
        base = (steps - 1 - turn) * (WIDE * count)
        observed = stacked(events, base, count)
        counts = jnp.dot(observed.astype(F32).astype(BF16), lower[...], preferred_element_type=F32)
        summed, totals = block_sums(stacked(weight, base, 2 * count, LANES), upper[...])
        for k in range(count - 1, -1, -1):
            mine = slice(k * rows, (k + 1) * rows)
            for half in (1, 0):
                lanes = slice(half * LANES, (half + 1) * LANES)
                at = span(base + k * WIDE + half * LANES, LANES)
                block = pl.ds((base + k * WIDE) // LANES + half, 1)
                here = slice((2 * k + half) * rows, (2 * k + half + 1) * rows)
                suffix[:, at] = summed[here] + carry
                carry = carry + totals[here]
                grouped[:, at] = group_events(
                    observed[mine, lanes],
                    counts[mine, lanes],
                    jnp.broadcast_to(tie[block, :], (rows // FIELDS, LANES)),
                    jnp.broadcast_to(last[block, :], (rows // FIELDS, LANES)),
                )
        return carry

    lax.fori_loop(0, steps, one, jnp.zeros((rows, LANES), F32), unroll=4)
    fetch.wait()


def pair_body(left, right, *refs):
    refs[-1][...] = left[...] + right[...]


def gathered_sum(meta, refs, later):
    mine = meta[1]
    out = None
    for k, ref in enumerate(refs):
        other = mine ^ (1 if k == 0 else 2 * k)
        wanted = (other > mine) if later else (other < mine)
        term = ref[...] * wanted.astype(F32)
        out = term if out is None else out + term
    return out


def inverse_body(count, parts, *refs):
    meta, others = refs[0], refs[1 : 1 + count]
    suffix, grouped, inv_one, inv_two, totals, after = refs[1 + count :]
    rows, length = suffix.shape
    share = length // parts
    later = gathered_sum(meta, others, True)
    for part in range(parts - 1):
        after[part] = jnp.broadcast_to(suffix[:, (part + 1) * share : (part + 1) * share + 1], (rows, LANES)) + later
    after[parts - 1] = later
    step = min(length, 512)

    def one(turn, acc):
        sum_one, sum_two = acc
        at = span(turn * step, step)
        inverse = 1.0 / (suffix[:, at] + widen(later, step))
        first = unpack(grouped[:, at]) * inverse
        second = first * inverse
        inv_one[:, at] = first
        inv_two[:, at] = second
        return (sum_one + fold(first), sum_two + fold(second))

    empty = jnp.zeros((rows, LANES), F32)
    sum_one, sum_two = lax.fori_loop(0, length // step, one, (empty, empty), unroll=4)
    totals[:rows, :] = lane_sum(sum_one)
    totals[rows:, :] = lane_sum(sum_two)


def accum_body(parts, inv_one, inv_two, one_out, two_out, before, lower):
    rows, length = inv_one.shape
    share = length // parts
    count = min(16, share // WIDE)
    lower[...] = scan_matrix(False)
    empty = jnp.zeros((rows, LANES), F32)
    carry = (empty, empty)
    for part in range(parts):
        before[part, :rows] = carry[0]
        before[part, rows:] = carry[1]

        def one(turn, carry):
            base = part * share + turn * (WIDE * count)
            made = []
            for ref, out, so_far in ((inv_one, one_out, carry[0]), (inv_two, two_out, carry[1])):
                summed, totals = block_sums(stacked(ref, base, 2 * count, LANES), lower[...])
                for k in range(2 * count):
                    mine = slice(k * rows, (k + 1) * rows)
                    out[:, span(base + k * LANES, LANES)] = summed[mine] + so_far
                    so_far = so_far + totals[mine]
                made.append(so_far)
            return tuple(made)

        carry = lax.fori_loop(0, share // (WIDE * count), one, carry, unroll=2)


def derivatives(weight, observed, accum_one, accum_two):
    scaled = weight * accum_one
    return scaled - observed, scaled - weight * weight * accum_two


def bases_body(count, links, *refs):
    meta, others = refs[0], refs[1 : 1 + count]
    after, before = refs[1 + count : 3 + count]
    bases, *messages = refs[len(refs) - 1 - len(links) :]
    rows = after.shape[1]
    earlier = gathered_sum(meta, others, False)
    bases[...] = earlier
    for d, message in zip(links, messages):
        part = share_of(meta, d, 1)
        message[:rows] = after[part]
        message[rows:] = before[part] + earlier


def release_body(*refs):
    pass


def place_pieces(meta, partners, arrived, out, sems):
    copies = []
    for k, (d, piece) in enumerate(zip(partners, arrived)):
        rows = piece.shape[1]
        where = pl.ds(pl.multiple_of(share_of(meta, d, rows), rows), rows)
        copies += [pltpu.make_async_copy(piece.at[v], out.at[v, where, :], sems.at[k, v]) for v in (0, 1)]
    return copies


def partner_scan(turn, slot, message, so_far, first_block, tie, last, upper, lower, kept, inv_one, inv_two):
    _, rows, share = kept.shape
    steps = share // PIECE
    count = PIECE // WIDE
    at_base = (steps - 1 - turn) * PIECE
    coded = jnp.concatenate([message[0, :, span(at_base + k * WIDE, WIDE)] for k in range(count)], axis=0)
    values = jnp.exp(coded.astype(jnp.int32).astype(F32) * (1.0 / CODE))
    seen = jnp.concatenate([message[1, :, span(at_base + k * WIDE, WIDE)] for k in range(count)], axis=0)
    observed = seen.astype(jnp.int32)
    counts = jnp.dot(observed.astype(F32).astype(BF16), lower[...], preferred_element_type=F32)
    blocks = [values[k * rows : (k + 1) * rows, half * LANES : (half + 1) * LANES] for k in range(count) for half in (0, 1)]
    summed, totals = block_sums(jnp.concatenate(blocks, axis=0), upper[...])
    for k in range(count - 1, -1, -1):
        mine = slice(k * rows, (k + 1) * rows)
        kept[slot, :, span(at_base + k * WIDE, WIDE)] = values[mine]
        for half in (1, 0):
            here = slice((2 * k + half) * rows, (2 * k + half + 1) * rows)
            lanes = slice(half * LANES, (half + 1) * LANES)
            at = span(at_base + k * WIDE + half * LANES, LANES)
            block = pl.ds(first_block + (at_base + k * WIDE) // LANES + half, 1)
            grouped = group_events(
                observed[mine, lanes],
                counts[mine, lanes],
                jnp.broadcast_to(tie[block, :], (rows // FIELDS, LANES)),
                jnp.broadcast_to(last[block, :], (rows // FIELDS, LANES)),
            )
            inverse = 1.0 / (summed[here] + so_far)
            so_far = so_far + totals[here]
            first = unpack(grouped) * inverse
            inv_one[slot, :, at] = first
            inv_two[slot, :, at] = first * inverse
    return so_far


def finish_body(partners, *refs):
    meta, refs = refs[0], refs[1:]
    messages, base = refs[: len(partners)], refs[len(partners) : 2 * len(partners)]
    own, kept, inv_one, inv_two, out, scratch, lower, sems, own_sems = refs[2 * len(partners) :]
    own_copies = place_pieces(meta, [0], [own], out, own_sems)
    for copy in own_copies:
        copy.start()
    _, rows, share = kept.shape
    steps = share // PIECE
    count = PIECE // WIDE
    lower[...] = scan_matrix(False)

    def copies(turn):
        lanes = span(turn * PIECE, PIECE)
        made = []
        for slot, d in enumerate(partners):
            where = pl.ds(pl.multiple_of(share_of(meta, d, rows), rows), rows)
            made += [
                pltpu.make_async_copy(scratch.at[slot, v, :, lanes], out.at[v, where, lanes], sems.at[slot, v, turn])
                for v in (0, 1)
            ]
        return made

    def one(turn, carry):
        at_base = turn * PIECE
        made = []
        for slot in range(len(partners)):
            sum_one, total_one = block_sums(stacked(inv_one.at[slot], at_base, 2 * count, LANES), lower[...])
            sum_two, total_two = block_sums(stacked(inv_two.at[slot], at_base, 2 * count, LANES), lower[...])
            so_one, so_two = carry[slot]
            for k in range(2 * count):
                mine = slice(k * rows, (k + 1) * rows)
                at = span(at_base + k * LANES, LANES)
                grad, hess = derivatives(
                    kept[slot, :, at],
                    messages[slot][1, :, at].astype(jnp.int32).astype(F32),
                    sum_one[mine] + so_one,
                    sum_two[mine] + so_two,
                )
                scratch[slot, 0, :, at] = grad.astype(BF16)
                scratch[slot, 1, :, at] = hess.astype(BF16)
                so_one = so_one + total_one[mine]
                so_two = so_two + total_two[mine]
            made.append((so_one, so_two))
        for copy in copies(turn):
            copy.start()
        return tuple(made)

    lax.fori_loop(0, steps, one, tuple((b[rows : 2 * rows, :], b[2 * rows :, :]) for b in base), unroll=2)
    for turn in range(steps):
        for copy in copies(turn):
            copy.wait()
    for copy in own_copies:
        copy.wait()


GROUP = 16
LOW = 16
HIGH = LEAVES // LOW


def leaf_step(at, leaf, weight, events, local_one, local_two, bases, acc, out, at_out):
    rows = weight.shape[0]
    step = at.size
    zero = jnp.zeros((GROUP, step), BF16)
    unit = jnp.ones((GROUP, step), BF16)
    for group in range(rows // GROUP):
        mine = pl.ds(group * GROUP, GROUP)
        pair = derivatives(
            weight[mine, at],
            events[mine, at].astype(F32),
            local_one[mine, at] + widen(bases[mine, :], step),
            local_two[mine, at] + widen(bases[pl.ds(rows + group * GROUP, GROUP), :], step),
        )
        label = leaf[mine, at]
        low = (label & (LOW - 1)).astype(F32).astype(BF16)
        high = lax.shift_right_logical(label, LOW.bit_length() - 1).astype(F32).astype(BF16)
        terms = []
        for value in pair:
            upper = value.astype(BF16)
            terms += [upper, (value - upper.astype(F32)).astype(BF16)]
        if out is not None:
            out[0, mine, at_out] = terms[0]
            out[1, mine, at_out] = terms[2]
        left = jnp.concatenate([jnp.where(high == h, term, zero) for term in terms for h in range(HIGH)], axis=0)
        right = jnp.concatenate([jnp.where(low == k, unit, zero) for k in range(LOW)], axis=0)
        acc[group] += lax.dot_general(left, right, (((1,), (1,)), ((), ())), preferred_element_type=F32)


def leaf_first_body(shares, size, meta, *refs):
    ins, outs, acc = refs[:6], refs[6:-1], refs[-1]
    acc[...] = jnp.zeros_like(acc)
    for d, out in zip(shares, outs):
        start = share_of(meta, d, size)

        def one(turn, carry):
            leaf_step(span(start + turn * PIECE, PIECE), *ins, acc, out, span(turn * PIECE, PIECE))
            return carry

        lax.fori_loop(0, size // PIECE, one, 0, unroll=4)


def leaf_rest_body(links, size, meta, *refs):
    ins, tie, last = refs[:6], refs[6], refs[7]
    messages, base = refs[8 : 8 + len(links)], refs[8 + len(links) : 8 + 2 * len(links)]
    pred_in = refs[-12]
    own, sums, kept, inv_one, inv_two, pred, acc, upper, lower, sem = refs[-10:]
    fetch = pltpu.make_async_copy(pred_in, pred, sem)
    fetch.start()
    upper[...] = scan_matrix(True)
    lower[...] = triangle(False)
    rows = kept.shape[1]
    first_block = share_of(meta, 0, size) // LANES

    def one(turn, carry):
        at = turn * PIECE
        made = []
        leaf_step(span(share_of(meta, 0, size) + at, PIECE), *ins, acc, own, span(at, PIECE))
        for slot, d in enumerate(links):
            made.append(
                partner_scan(
                    turn, slot, messages[slot], carry[slot], first_block, tie, last, upper, lower, kept, inv_one, inv_two
                )
            )
            leaf_step(span(share_of(meta, d, size) + at, PIECE), *ins, acc, None, None)
        return tuple(made)

    lax.fori_loop(0, size // PIECE, one, tuple(b[:rows, :] for b in base), unroll=2)
    width = LOW * GROUP
    side = HIGH * GROUP
    same = lax.broadcasted_iota(jnp.int32, (side, width), 0) % GROUP == lax.broadcasted_iota(jnp.int32, (side, width), 1) % GROUP
    held = []
    for group in range(rows // GROUP):
        for value in (0, 1):
            both = acc[group, 2 * value * side : (2 * value + 1) * side] + acc[group, (2 * value + 1) * side : (2 * value + 2) * side]
            held.append(jnp.where(same, both, 0.0))
    held = jnp.concatenate(held, axis=0)
    source = lax.broadcasted_iota(jnp.int32, (width, LANES), 0) // GROUP
    place = (source == lax.broadcasted_iota(jnp.int32, (width, LANES), 1)).astype(BF16)
    by_low = jnp.zeros((held.shape[0], LANES), F32)
    for _ in range(3):
        part = held.astype(BF16)
        held = held - part.astype(F32)
        by_low = by_low + jnp.dot(part, place, preferred_element_type=F32)
    for group in range(rows // GROUP):
        out = jnp.zeros((GROUP, LANES), F32)
        for value in (0, 1):
            for h in range(HIGH):
                at = ((group * 2 + value) * HIGH + h) * GROUP
                out = out + pltpu.roll(by_low[at : at + GROUP], h * LOW + value * LEAVES, 1)
        sums[group * GROUP : (group + 1) * GROUP, :] = out
    fetch.wait()


def place_body(partners, cuts, meta, *refs):
    out, sems = refs[-2:]
    copies = []
    for k, (d, piece) in enumerate(zip(partners, refs)):
        _, rows, size = piece.shape
        where = pl.ds(pl.multiple_of(share_of(meta, d, rows), rows), rows)
        for v in (0, 1):
            for cut in range(cuts):
                lanes = pl.ds(cut * (size // cuts), size // cuts)
                copies.append(pltpu.make_async_copy(piece.at[v, :, lanes], out.at[v, where, lanes], sems.at[k, v, cut]))
    for copy in copies:
        copy.start()
    for copy in copies:
        copy.wait()


def update_body(turns, pred, leaf, *refs):
    sums, (new_pred, leaf_weights, scratch, weights, sems) = refs[:-5], refs[-5:]
    rows, length = leaf.shape
    both = [ref[...] for ref in sums]
    while len(both) > 1:
        both = [a + b for a, b in zip(both[::2], both[1::2])]
    table = -both[0] / (pltpu.roll(both[0], LANES - LEAVES, 1) + 1.0)
    weights[...] = table[:, :LEAVES]
    copies = [pltpu.make_async_copy(weights, leaf_weights, sems.at[turns])]
    copies[0].start()
    width = length // turns
    step = min(width, 512)
    for turn in range(turns):

        def one(k, carry):
            at = span(turn * width + k * step, step)
            label = leaf[:, at]
            picked = [take(table, label[:, j : j + LANES]) for j in range(0, step, LANES)]
            scratch[:, at] = pred[:, at] + jnp.concatenate(picked, axis=1)
            return carry

        lax.fori_loop(0, width // step, one, 0, unroll=8)
        at = pl.ds(turn * width, width)
        copies.append(pltpu.make_async_copy(scratch.at[:, at], new_pred.at[:, at], sems.at[turn]))
        copies[-1].start()
    for copy in copies:
        copy.wait()


def swap(array, axis, d):
    return lax.ppermute(array, axis, [(i, i ^ d) for i in range(lax.axis_size(axis))])


def across(total, axis, arrived=()):
    mate = swap(total, axis, 1)
    (both,) = call(pair_body, [resident(total.shape, F32)], total, mate, *arrived, name="pair", us=0.3, limit=4)
    return both, [mate] + [swap(both, axis, d) for d in range(2, lax.axis_size(axis), 2)]


def on_device(predictions, leaf_index, events, tie_start):
    rows, length = predictions.shape
    blocks = length // LANES
    parts = lax.axis_size("ep")
    share = length // parts
    wide = (rows, length)
    turns = 8
    dma = pltpu.SemaphoreType.DMA
    tie = near(tie_start.reshape(blocks, LANES))
    meta = jnp.stack([lax.axis_index("ep"), lax.axis_index("tm")]).astype(jnp.int32)

    links = [d for d in range(1, parts) if d & (d - 1) == 0]
    diagonals = [d for d in range(1, parts) if d not in links]
    message = resident((2, rows, share), I16)
    observed, weight, total, *messages = call(
        functools.partial(front_body, links, turns, parts),
        [resident(wide, jnp.int32), resident(wide, F32), resident((rows, LANES), F32)] + [message] * len(links),
        meta,
        far(predictions),
        far(events),
        hbm=(1, 2),
        scratch=[pltpu.VMEM(wide, F32), dma((turns,)), dma((parts,))],
        name="front",
        us=4,
    )
    coded = {d: swap(m, "ep", d) for d, m in zip(links, messages)}
    _, from_later = across(total, "tm")
    suffix, grouped, last, leaf = call(
        scan_body,
        [
            resident(wide, F32),
            resident((rows // FIELDS, length), jnp.int32),
            resident((blocks, LANES), jnp.int32),
            resident(wide, jnp.int32),
        ],
        weight,
        observed,
        tie,
        far(leaf_index),
        hbm=(3,),
        scratch=[pltpu.VMEM((WIDE, WIDE), BF16)] * 2 + [dma],
        name="scan",
        us=5,
    )
    count = len(from_later)
    inv_one, inv_two, totals, after = call(
        functools.partial(inverse_body, count, parts),
        [resident(wide, F32), resident(wide, F32), resident((2 * rows, LANES), F32), resident((parts, rows, LANES), F32)],
        meta,
        *from_later,
        suffix,
        grouped,
        aliases={1 + count: 0},
        name="inverse",
        us=1.5,
    )
    _, from_earlier = across(totals, "tm")
    local_one, local_two, before = call(
        functools.partial(accum_body, parts),
        [resident(wide, F32), resident(wide, F32), resident((parts, 2 * rows, LANES), F32)],
        inv_one,
        inv_two,
        aliases={0: 0, 1: 1},
        scratch=[pltpu.VMEM((WIDE, WIDE), BF16)],
        name="accum",
        us=3,
    )
    scans = (weight, observed, local_one, local_two)
    bases, *sent = call(
        functools.partial(bases_body, count, links),
        [resident((2 * rows, LANES), F32)] + [resident((3 * rows, LANES), F32)] * len(links),
        meta,
        *from_earlier,
        after,
        before,
        name="bases",
        us=1,
    )
    base = {d: swap(m, "ep", d) for d, m in zip(links, sent)}
    finished = resident((2, rows, share), BF16)
    sums_shape = resident((rows // GROUP, 4 * HIGH * GROUP, LOW * GROUP), F32)
    *sent, acc = call(
        functools.partial(leaf_first_body, diagonals, share),
        [finished] * len(diagonals) + [sums_shape],
        meta,
        leaf,
        *scans,
        bases,
        name="leaf_first",
        us=3,
    )
    sent = call(
        release_body,
        [finished] * len(diagonals),
        *sent,
        *base.values(),
        *coded.values(),
        aliases={k: k for k in range(len(diagonals))},
        name="release",
        us=0.1,
        limit=2,
    )
    arrived = [swap(m, "ep", d) for d, m in zip(diagonals, sent)]
    piece = resident((len(links), rows, share), F32)
    received = [*[coded[d] for d in links], *[base[d] for d in links]]
    args = [meta, leaf, *scans, bases, tie, last, *received]
    own, own_sums, *held, pred, _ = call(
        functools.partial(leaf_rest_body, links, share),
        [finished, resident((rows, LANES), F32)] + [piece] * 3 + [resident(wide, F32), sums_shape],
        *args,
        acc,
        *sent,
        far(predictions),
        bases,
        hbm=(len(args) + 1 + len(sent),),
        aliases={len(args): 6},
        scratch=[pltpu.VMEM((WIDE, WIDE), BF16)] * 2 + [dma],
        name="leaf_rest",
        us=10,
    )
    both, others = across(own_sums, "tm", base.values())
    args = [meta, *received, own, *held]
    (grad_hess,) = call(
        functools.partial(finish_body, links),
        [jax.ShapeDtypeStruct((2, rows * parts, share), BF16)],
        *args,
        hbm_out=(0,),
        scratch=[
            pltpu.VMEM((len(links), 2, rows, share), BF16),
            pltpu.VMEM((WIDE, WIDE), BF16),
            dma((len(links), 2, share // PIECE)),
            dma((1, 2)),
        ],
        name="finish",
        us=4,
    )
    new_pred, leaf_weights = call(
        functools.partial(update_body, turns),
        [jax.ShapeDtypeStruct(wide, F32), jax.ShapeDtypeStruct((rows, LEAVES), F32)],
        pred,
        leaf,
        both,
        *others[1:],
        hbm_out=(0, 1),
        scratch=[pltpu.VMEM(wide, F32), pltpu.VMEM((rows, LEAVES), F32), dma((turns + 1,))],
        name="update",
        us=4,
    )
    cuts = 4
    (grad_hess,) = call(
        functools.partial(place_body, diagonals, cuts),
        [jax.ShapeDtypeStruct(grad_hess.shape, BF16)],
        meta,
        *[near(x) for x in arrived],
        grad_hess,
        far(new_pred),
        hbm=(1 + len(arrived), 2 + len(arrived)),
        hbm_out=(0,),
        aliases={1 + len(arrived): 0},
        scratch=[dma((max(1, len(arrived)), 2, cuts))],
        name="place",
        us=1,
        limit=2,
    )
    return new_pred, leaf_weights, grad_hess.reshape(2, rows * parts, 1, share)


def solution(mesh):
    placed = (P("ep", "tm"), P("ep", "tm"), P("ep", "tm"), P("tm"))
    return jax.shard_map(
        on_device,
        mesh=mesh,
        in_specs=placed,
        out_specs=(P("ep", "tm"), P("ep", None), P(None, None, "tm", "ep")),
        check_vma=False,
    )
```
